128 devices in a mesh: expert: 64 (over z, y, x), node: 2 (over core).
Axes of the slice: x: 4, y: 4, z: 4, core: 2. Of those that a mesh axis runs over, the one named last changes fastest.
Arguments:
- samples: bfloat16 [98304, 512], P(('expert', 'node')), may hold values from -6 to 6
- cotangent: bfloat16 [98304, 512], P(('expert', 'node')), may hold values from -6 to 6
- weights: bfloat16 [256, 2, 512, 512], P('expert', None, 'node'), may hold values from -0.25 to 0.25
- expert_ids: int32 [98304, 1], P(('expert', 'node')), may hold values from 0 to 255; in each aligned block of 768 rows (0 to 767, 768 to 1535, ...) at most 6 rows name the same one
Outputs:
- sample_grads: bfloat16 [98304, 512], P(('expert', 'node'))
- weight_grads: bfloat16 [256, 2, 512, 512], P('expert', None, 'node')
The draws below stay inside these ranges and needn't reach their ends.
Inputs may be any that keep to these rules, and one draw needn't show every extreme that they name: `expert_ids`: among the samples of one device no expert is named more than 6 times, and in some device's samples one expert is named exactly 6 times.
All inputs are finite; a program needn't handle non-finite values.
Results may differ from the reference program's by a relative error of at most 0.015.
Values may be sent and summed in bfloat16 or wider, within the bound.
A program may use at most 64 MiB of HBM per device.

```python
import math
import jax
import jax.numpy as jnp
import numpy as np
from jax import lax

D = 512
LAYERS = 2
EXP_DEV = 4
SAMP_DEV = 768
EXPERTS = 256
CAP = 6
SAMPLES = 98304
N_EXPERT = 64
N_NODE = 2


def steps_of(rng, shape, shards, least, high):
    loudness = 1.0
    for dim, shards_of in shards:
        draws = jax.random.uniform(jax.random.fold_in(jax.random.fold_in(rng, 6), dim), (shards_of,), jnp.float32, least / len(shards), high / len(shards))
        loudness = loudness * jnp.repeat(jnp.exp(draws), shape[dim] // shards_of).reshape((-1,) + (1,) * (len(shape) - 1 - dim))
    return loudness


def deal_out(key, own, number, rows, number_of, top, reach, slope):
    order = jax.random.permutation(key, number_of)
    crowded, usual = load_shares(number_of, rows * top, reach, slope, True), load_shares(number_of, rows * top, reach, slope, False)
    places = jnp.arange(number_of)

    def named(lengths, rotation):
        used = int((lengths > 0).sum())
        fixed = max(1, used // 4)
        passed = fixed + (places - fixed + rotation * (used - fixed)) % max(1, number_of - fixed)
        return jnp.zeros((number_of,), jnp.int32).at[order[jnp.where(places < fixed, places, passed)]].set(jnp.asarray(lengths, jnp.int32))

    lengths = jnp.where(number % 4 == 0, named(crowded, number // 4), named(usual, number - number // 4 - 1))
    mixed = jax.random.permutation(jax.random.fold_in(own, 3), number_of)
    donor, receiver = mixed[0:number_of // 2 * 2:2], mixed[1:number_of // 2 * 2:2]
    margin = jnp.minimum(lengths[donor] - 1, reach - lengths[receiver]) // 2
    margin = jnp.where((donor == order[0]) | (receiver == order[0]) | (lengths[receiver] == 0), 0, jnp.maximum(margin, 0))
    passed = jax.random.randint(jax.random.fold_in(own, 4), (number_of // 2,), 0, 1 << 20) % (margin + 1)
    lengths = lengths.at[donor].add(-passed).at[receiver].add(passed)
    labels = jnp.searchsorted(jnp.cumsum(lengths), jnp.arange(rows * top), side="right").astype(jnp.int32)
    listing = labels.reshape(top, rows).T
    listing = listing[jax.random.permutation(jax.random.fold_in(own, 1), rows)]
    rotation = jax.random.randint(jax.random.fold_in(own, 2), (rows, 1), 0, top)
    return jnp.take_along_axis(listing, (jnp.arange(top)[None, :] + rotation) % top, axis=1)


def load_shares(amount, total, most, lean, full):
    portions = [(1 << 20) // math.isqrt(standing ** lean) + 1 for standing in range(1, amount + 1)]
    largest = most if full else min(most, max(-(-total // amount), total * portions[0] // sum(portions)))
    least = 1 if total - largest >= amount - 1 else 0
    holding, surplus = [largest] + [least] * (amount - 1), total - largest - least * (amount - 1)
    while surplus > 0:
        candidates = [i for i in range(1, amount) if holding[i] < largest] or [i for i in range(1, amount) if holding[i] < most]
        mass, remaining = sum([portions[i] for i in candidates]), surplus
        for i in candidates:
            more = min(most - holding[i], max(1, remaining * portions[i] // mass), surplus)
            holding[i] = holding[i] + more
            surplus = surplus - more
    return np.array(holding)


def scatter_about(stream_key, shape, spread, most, pieces=(), kind=jnp.bfloat16):
    drawn = jax.random.normal(stream_key, shape, jnp.float32) * spread
    if len(pieces) > 0:
        drawn = steps_of(stream_key, shape, pieces, -0.22, 0.18) * drawn
    return jnp.clip(drawn, min=-most, max=most).astype(kind)


def setup_inputs(seed: int = 0) -> dict:
    key_list = jax.random.split(jax.random.key(seed), 5)
    samples = scatter_about(key_list[0], (SAMPLES, D), 1.0, 6.0, ((0, 128),))
    cotangent = scatter_about(key_list[1], (SAMPLES, D), 1.0, 6.0, ((0, 128),))
    weights = scatter_about(key_list[2], (EXPERTS, LAYERS, D, D), D ** -0.5, 0.25, ((0, 64), (2, 2)))
    expert_ids_keys = jax.random.split(jax.random.fold_in(key_list[3], 1), SAMPLES // SAMP_DEV)
    expert_ids_turns = jax.random.permutation(jax.random.fold_in(key_list[3], 3), SAMPLES // SAMP_DEV)
    expert_ids = jax.vmap(lambda own, number: deal_out(jax.random.fold_in(key_list[3], 2), own, number, SAMP_DEV, EXPERTS, 1, CAP, 2))(expert_ids_keys, expert_ids_turns).reshape((SAMPLES, 1))
    return dict(samples=samples, cotangent=cotangent, weights=weights, expert_ids=expert_ids)


def silu_slope(preact):
    sigmoid_val = jax.nn.sigmoid(preact)
    return sigmoid_val * (1.0 + preact * (1.0 - sigmoid_val))

def reference(samples, cotangent, weights, expert_ids):
    owner_count = N_EXPERT
    node_count = N_NODE
    sample_count = owner_count * node_count * SAMP_DEV
    expert_of = expert_ids[:, 0].astype(jnp.int32)
    blocks = expert_of.reshape(owner_count * node_count, SAMP_DEV)

    def count_slots(device_ids):
        onehot = (device_ids[:, None] == jnp.arange(EXPERTS, dtype=jnp.int32)[None, :]).astype(jnp.int32)
        before = jnp.cumsum(onehot, axis=0) - onehot
        return lax.optimization_barrier(jnp.sum(before * onehot, axis=1)).astype(jnp.int32)
    slot_of = lax.map(count_slots, blocks).reshape(sample_count)
    device = jnp.arange(sample_count, dtype=jnp.int32) // SAMP_DEV
    source_owner = device // node_count
    source_node = device % node_count
    slot_table = jnp.full((node_count, EXPERTS, owner_count, CAP), sample_count, jnp.int32)
    slot_table = slot_table.at[source_node, expert_of, source_owner, slot_of].set(jnp.arange(sample_count, dtype=jnp.int32))
    x_pad = jnp.concatenate([samples, jnp.zeros((1, D), samples.dtype)], 0)
    g_pad = jnp.concatenate([cotangent, jnp.zeros((1, D), cotangent.dtype)], 0)
    norm_scale = 1.0 / math.sqrt(SAMP_DEV * node_count / EXP_DEV)

    def per_expert(grad_rows, expert):
        row_index = slot_table[:, expert].reshape(node_count * owner_count * CAP)
        row_feats = x_pad[row_index]
        row_cots = g_pad[row_index]
        weight = weights[expert]
        acts = [row_feats]
        preacts = []
        for layer in range(LAYERS):
            preact = jnp.dot(acts[-1], weight[layer], preferred_element_type=jnp.float32)
            preacts.append(preact)
            if layer < LAYERS - 1:
                acts.append(jax.nn.silu(preact).astype(jnp.bfloat16))
        grad = row_cots
        partials = [None] * LAYERS
        for layer in reversed(range(LAYERS)):
            pre_grad = (grad.astype(jnp.float32) * silu_slope(preacts[layer])).astype(jnp.bfloat16)
            feats_node = acts[layer].reshape(node_count, owner_count * CAP, D).astype(jnp.float32)
            grads_node = pre_grad.reshape(node_count, owner_count * CAP, D).astype(jnp.float32)
            partial_value = jnp.einsum('nrd,nrk->ndk', feats_node, grads_node) * norm_scale
            partial_value = lax.optimization_barrier(partial_value.astype(jnp.bfloat16)).astype(jnp.float32)
            partials[layer] = lax.optimization_barrier(jnp.sum(partial_value, axis=0)).astype(jnp.bfloat16)
            grad = jnp.dot(pre_grad, weight[layer].T, preferred_element_type=jnp.float32).astype(jnp.bfloat16)
        grad_rows = grad_rows.at[row_index].set(grad)
        return (grad_rows, jnp.stack(partials, 0))
    grad_rows, weight_grads = lax.scan(per_expert, jnp.zeros((sample_count + 1, D), jnp.bfloat16), jnp.arange(EXPERTS, dtype=jnp.int32))
    return (grad_rows[:sample_count], weight_grads)
```

```python
import functools
import math

import jax
import jax.numpy as jnp
import numpy as np
from jax import lax
from jax.experimental import pallas as pl
from jax.experimental.pallas import tpu as pltpu
from jax.sharding import PartitionSpec as P

MESH = pl.DeviceIdType.MESH
ROWS = 768
FEAT = 512
HALF = 256
EXPERTS = 256
LOCAL = 4
CAP = 6
PAIR = LOCAL * CAP
MSG = 2 * PAIR
PEERS = 64
GROUP = 16
GROUPS = PEERS // GROUP
BLOCK = 8
BLOCKS = GROUP // BLOCK
GROUP_ROWS = GROUP * CAP
EXPERT_ROWS = PEERS * CAP


def sort_matrices():
    into = np.zeros((BLOCK * MSG, BLOCK * MSG), np.float32)
    back = np.zeros((BLOCK * PAIR, BLOCK * PAIR), np.float32)
    for msg in range(BLOCK):
        for kind in range(2):
            for local in range(LOCAL):
                for slot in range(CAP):
                    by_expert = local * BLOCK * CAP + msg * CAP + slot
                    by_message = local * CAP + slot
                    into[kind * BLOCK * PAIR + by_expert, msg * MSG + kind * PAIR + by_message] = 1
                    if kind == 0:
                        back[msg * PAIR + by_message, by_expert] = 1
    return into, back


def dot(a, b):
    return jnp.dot(a, b, preferred_element_type=jnp.float32)


def dot_t(a, b):
    return lax.dot_general(a, b, (((1,), (1,)), ((), ())), preferred_element_type=jnp.float32)


def t_dot(a, b):
    return lax.dot_general(a, b, (((0,), (0,)), ((), ())), preferred_element_type=jnp.float32)


def kernel(
    norm_scale,
    ids_ref,
    into_ref,
    back_ref,
    samples_ref,
    cot_ref,
    weights_ref,
    grads_ref,
    wgrads_ref,
    send_buf,
    recv_buf,
    ysend_buf,
    yrecv_buf,
    x_group,
    g_group,
    y_group,
    act0,
    act1,
    pre0,
    pre1,
    wfull,
    wg_own,
    wg_send,
    wg_recv,
    target_col,
    acc,
    send_sem,
    recv_sem,
    ysend_sem,
    yrecv_sem,
    wlocal_sem,
    wsend_sem,
    wrecv_sem,
    gsend_sem,
    grecv_sem,
):
    me = lax.axis_index("expert")
    node = lax.axis_index("node")
    my_x = lax.rem(me, 4)
    my_y = lax.rem(lax.div(me, 4), 4)
    my_z = lax.div(me, 16)

    def shifted(pos, sign):
        dx = lax.rem(pos, 4)
        dy = lax.rem(lax.div(pos, 4), 4)
        dz = lax.rem(lax.div(pos, 16) + dx + dy, 4)
        px = lax.rem(my_x + sign * dx + 4, 4)
        py = lax.rem(my_y + sign * dy + 4, 4)
        pz = lax.rem(my_z + sign * dz + 4, 4)
        return pz * 16 + py * 4 + px

    barrier = pltpu.get_barrier_semaphore()

    def greet(pos, carry):
        pl.semaphore_signal(
            barrier, inc=1, device_id=(shifted(pos, 1), node), device_id_type=MESH
        )
        return carry

    lax.fori_loop(1, PEERS, greet, 0)
    pl.semaphore_signal(barrier, inc=1, device_id=(me, 1 - node), device_id_type=MESH)

    my_half = pl.ds(pl.multiple_of(node * HALF, HALF), HALF)
    w_local = pltpu.make_async_copy(weights_ref, wfull.at[:, :, my_half, :], wlocal_sem)
    w_local.start()
    w_remote = pltpu.make_async_remote_copy(
        src_ref=weights_ref,
        dst_ref=wfull.at[:, :, my_half, :],
        send_sem=wsend_sem,
        recv_sem=wrecv_sem,
        device_id=(me, 1 - node),
        device_id_type=MESH,
    )

    ids = ids_ref[...]
    onehot = lax.broadcasted_iota(jnp.int32, (EXPERTS, ROWS), 0) == ids
    before = lax.broadcasted_iota(jnp.int32, (ROWS, ROWS), 0) < lax.broadcasted_iota(
        jnp.int32, (ROWS, ROWS), 1
    )
    earlier = dot(onehot.astype(jnp.bfloat16), before.astype(jnp.bfloat16))
    slot = jnp.sum(jnp.where(onehot, earlier, 0.0), axis=0, keepdims=True).astype(jnp.int32)
    owner = ids >> 2
    dx = ((owner & 3) - my_x + 4) & 3
    dy = (((owner >> 2) & 3) - my_y + 4) & 3
    dz = ((owner >> 4) - my_z + 4) & 3
    pos_of = ((dz - dx - dy + 8) & 3) * 16 + dy * 4 + dx
    target = pos_of * PAIR + (ids & 3) * CAP + slot
    target_col[...] = jnp.broadcast_to(target.astype(jnp.float32), (128, ROWS)).T

    def message(pos):
        return pltpu.make_async_remote_copy(
            src_ref=send_buf.at[pos],
            dst_ref=recv_buf.at[pos],
            send_sem=send_sem.at[pos],
            recv_sem=recv_sem.at[pos],
            device_id=(shifted(pos, 1), node),
            device_id_type=MESH,
        )

    def reply(pos):
        return pltpu.make_async_remote_copy(
            src_ref=ysend_buf.at[pos],
            dst_ref=yrecv_buf.at[pos],
            send_sem=ysend_sem.at[pos],
            recv_sem=yrecv_sem.at[pos],
            device_id=(shifted(pos, -1), node),
            device_id_type=MESH,
        )

    def over(low, high, action):
        def step(pos, carry):
            action(pos)
            return carry

        lax.fori_loop(low, high, step, 0)

    def first_of(group):
        return jnp.where(group == 0, 1, group * GROUP)

    pl.semaphore_wait(barrier, PEERS)

    def dispatch(group, carry):
        rows = lax.broadcasted_iota(jnp.int32, (GROUP * PAIR, ROWS), 0) + group * (GROUP * PAIR)
        pick = (rows == target).astype(jnp.bfloat16)
        feats = dot(pick, samples_ref[...])
        cots = dot(pick, cot_ref[...])
        for j in range(GROUP):
            part = slice(j * PAIR, (j + 1) * PAIR)
            both = jnp.concatenate([feats[part], cots[part]], 0).astype(jnp.bfloat16)
            send_buf[group * GROUP + j] = both
            if j == 0:

                @pl.when(group == 0)
                def _():
                    recv_buf[0] = both

        over(first_of(group), (group + 1) * GROUP, lambda pos: message(pos).start())

        @pl.when(group == 0)
        def _():
            w_remote.start()

        return carry

    lax.fori_loop(0, GROUPS, dispatch, 0)
    w_local.wait()
    w_remote.wait()

    def slope(val, sig):
        return sig * (1.0 + val * (1.0 - sig))

    def compute(group, carry):
        over(first_of(group), (group + 1) * GROUP, lambda pos: message(pos).wait_recv())
        for block in range(BLOCKS):
            start = group * GROUP + block * BLOCK
            received = recv_buf[pl.ds(start, BLOCK)].reshape(BLOCK * MSG, FEAT)
            ordered = dot(into_ref[...], received).astype(jnp.bfloat16)
            size = BLOCK * CAP
            for local in range(LOCAL):
                x_group[local, block * size : (block + 1) * size] = ordered[
                    local * size : (local + 1) * size
                ]
                g_group[local, block * size : (block + 1) * size] = ordered[
                    BLOCK * PAIR + local * size : BLOCK * PAIR + (local + 1) * size
                ]
        rows = pl.ds(pl.multiple_of(group * GROUP_ROWS, GROUP_ROWS), GROUP_ROWS)

        def expert(local, inner):
            feats = x_group[local]
            act0[local, rows] = feats
            val0 = dot(feats, wfull[local, 0])
            sig0 = jax.nn.sigmoid(val0)
            hidden = (val0 * sig0).astype(jnp.bfloat16)
            act1[local, rows] = hidden
            val1 = dot(hidden, wfull[local, 1])
            sig1 = jax.nn.sigmoid(val1)
            grad1 = (g_group[local].astype(jnp.float32) * slope(val1, sig1)).astype(jnp.bfloat16)
            pre1[local, rows] = grad1
            back1 = dot_t(grad1, wfull[local, 1]).astype(jnp.bfloat16).astype(jnp.float32)
            grad0 = (back1 * slope(val0, sig0)).astype(jnp.bfloat16)
            pre0[local, rows] = grad0
            y_group[local] = dot_t(grad0, wfull[local, 0]).astype(jnp.bfloat16)
            return inner

        lax.fori_loop(0, LOCAL, expert, 0)
        for block in range(BLOCKS):
            size = BLOCK * CAP
            by_expert = y_group[:, block * size : (block + 1) * size].reshape(BLOCK * PAIR, FEAT)
            by_message = dot(back_ref[...], by_expert)
            for j in range(BLOCK):
                part = slice(j * PAIR, (j + 1) * PAIR)
                both = jnp.concatenate([by_message[part, :HALF], by_message[part, HALF:]], 0)
                both = both.astype(jnp.bfloat16)
                ysend_buf[group * GROUP + block * BLOCK + j] = both
                if block == 0 and j == 0:

                    @pl.when(group == 0)
                    def _():
                        yrecv_buf[0] = both

        over(first_of(group), (group + 1) * GROUP, lambda pos: reply(pos).start())
        return carry

    lax.fori_loop(0, GROUPS, compute, 0)

    other_half = pl.ds(pl.multiple_of((1 - node) * HALF, HALF), HALF)

    def wg_copy(local):
        return pltpu.make_async_remote_copy(
            src_ref=wg_send.at[local],
            dst_ref=wg_recv.at[local],
            send_sem=gsend_sem.at[local],
            recv_sem=grecv_sem.at[local],
            device_id=(me, 1 - node),
            device_id_type=MESH,
        )

    def weight_grads(local, carry):
        for layer, (act, pre) in enumerate(((act0, pre0), (act1, pre1))):
            grad = pre[local]
            sent = t_dot(act[local, :, other_half], grad) * norm_scale
            wg_send[local, layer] = sent.astype(jnp.bfloat16)
            kept = t_dot(act[local, :, my_half], grad) * norm_scale
            wg_own[local, layer] = kept.astype(jnp.bfloat16)
        wg_copy(local).start()
        return carry

    lax.fori_loop(0, LOCAL, weight_grads, 0)

    def add_grads(local, carry):
        wg_copy(local).wait()
        total = wg_own[local].astype(jnp.float32) + wg_recv[local].astype(jnp.float32)
        wgrads_ref[local] = total.astype(jnp.bfloat16)
        return carry

    lax.fori_loop(0, LOCAL, add_grads, 0)

    acc[...] = jnp.zeros_like(acc)

    def combine(group, carry):
        over(first_of(group), (group + 1) * GROUP, lambda pos: reply(pos).wait_recv())
        received = yrecv_buf[pl.ds(group * GROUP, GROUP)].astype(jnp.float32)
        left = received[:, :PAIR].reshape(GROUP * PAIR, HALF)
        right = received[:, PAIR:].reshape(GROUP * PAIR, HALF)
        ordered = jnp.concatenate([left, right], 1).astype(jnp.bfloat16)
        columns = lax.broadcasted_iota(jnp.int32, (ROWS, GROUP * PAIR), 1) + group * (GROUP * PAIR)
        pick = (target_col[:, :1].astype(jnp.int32) == columns).astype(jnp.bfloat16)
        acc[...] += dot(pick, ordered)
        return carry

    lax.fori_loop(0, GROUPS, combine, 0)
    grads_ref[...] = acc[...].astype(jnp.bfloat16)

    over(1, PEERS, lambda pos: message(pos).wait_send())
    over(1, PEERS, lambda pos: reply(pos).wait_send())


def on_device(samples, cotangent, weights, expert_ids):
    bf16 = jnp.bfloat16
    into, back = sort_matrices()
    node_count = lax.axis_size("node")
    norm_scale = 1.0 / math.sqrt(ROWS * node_count / LOCAL)
    vmem = pl.BlockSpec(memory_space=pltpu.VMEM)
    return pl.pallas_call(
        functools.partial(kernel, norm_scale),
        out_shape=(
            jax.ShapeDtypeStruct((ROWS, FEAT), bf16),
            jax.ShapeDtypeStruct((LOCAL, 2, HALF, FEAT), bf16),
        ),
        in_specs=[vmem] * 5 + [pl.BlockSpec(memory_space=pl.ANY)],
        out_specs=(vmem, vmem),
        scratch_shapes=[
            pltpu.VMEM((PEERS, MSG, FEAT), bf16),
            pltpu.VMEM((PEERS, MSG, FEAT), bf16),
            pltpu.VMEM((PEERS, MSG, HALF), bf16),
            pltpu.VMEM((PEERS, MSG, HALF), bf16),
            pltpu.VMEM((LOCAL, GROUP_ROWS, FEAT), bf16),
            pltpu.VMEM((LOCAL, GROUP_ROWS, FEAT), bf16),
            pltpu.VMEM((LOCAL, GROUP_ROWS, FEAT), bf16),
            pltpu.VMEM((LOCAL, EXPERT_ROWS, FEAT), bf16),
            pltpu.VMEM((LOCAL, EXPERT_ROWS, FEAT), bf16),
            pltpu.VMEM((LOCAL, EXPERT_ROWS, FEAT), bf16),
            pltpu.VMEM((LOCAL, EXPERT_ROWS, FEAT), bf16),
            pltpu.VMEM((LOCAL, 2, FEAT, FEAT), bf16),
            pltpu.VMEM((LOCAL, 2, HALF, FEAT), bf16),
            pltpu.VMEM((LOCAL, 2, HALF, FEAT), bf16),
            pltpu.VMEM((LOCAL, 2, HALF, FEAT), bf16),
            pltpu.VMEM((ROWS, 128), jnp.float32),
            pltpu.VMEM((ROWS, FEAT), jnp.float32),
            pltpu.SemaphoreType.DMA((PEERS,)),
            pltpu.SemaphoreType.DMA((PEERS,)),
            pltpu.SemaphoreType.DMA((PEERS,)),
            pltpu.SemaphoreType.DMA((PEERS,)),
            pltpu.SemaphoreType.DMA,
            pltpu.SemaphoreType.DMA,
            pltpu.SemaphoreType.DMA,
            pltpu.SemaphoreType.DMA((LOCAL,)),
            pltpu.SemaphoreType.DMA((LOCAL,)),
        ],
        compiler_params=pltpu.CompilerParams(
            collective_id=0, has_side_effects=True, vmem_limit_bytes=52 * 1024 * 1024
        ),
    )(
        expert_ids.reshape(1, ROWS),
        jnp.asarray(into, bf16),
        jnp.asarray(back, bf16),
        samples,
        cotangent,
        weights,
    )


def solution(mesh):
    return jax.shard_map(
        on_device,
        mesh=mesh,
        in_specs=(
            P(("expert", "node"), None),
            P(("expert", "node"), None),
            P("expert", None, "node", None),
            P(("expert", "node"), None),
        ),
        out_specs=(P(("expert", "node"), None), P("expert", None, "node", None)),
        check_vma=False,
    )
```

```python
import functools
import math

import jax
import jax.numpy as jnp
from jax import lax
from jax.experimental import pallas as pl
from jax.experimental.pallas import tpu as pltpu
from jax.sharding import PartitionSpec as P

MESH = pl.DeviceIdType.MESH
ROWS = 768
FEAT = 512
HALF = 256
EXPERTS = 256
LOCAL = 4
CAP = 6
PAIR = LOCAL * CAP
MSG = 2 * PAIR
PEERS = 64
GROUP = 16
GROUPS = PEERS // GROUP
BLOCK = 8
BLOCKS = GROUP // BLOCK
GROUP_ROWS = GROUP * CAP
EXPERT_ROWS = PEERS * CAP


def sort_matrix():
    size = BLOCK * MSG
    row = lax.broadcasted_iota(jnp.int32, (1, size), 1)
    msg = sum((row >= (k + 1) * MSG).astype(jnp.int32) for k in range(BLOCK - 1))
    rest = row - msg * MSG
    kind = (rest >= PAIR).astype(jnp.int32)
    rest = rest - kind * PAIR
    local = sum((rest >= (k + 1) * CAP).astype(jnp.int32) for k in range(LOCAL - 1))
    slot = rest - local * CAP
    place = kind * (BLOCK * PAIR) + local * (BLOCK * CAP) + msg * CAP + slot
    return (lax.broadcasted_iota(jnp.int32, (size, size), 0) == place).astype(jnp.bfloat16)


def unsort_matrix():
    size = BLOCK * PAIR
    row = lax.broadcasted_iota(jnp.int32, (1, size), 1)
    local = sum((row >= (k + 1) * BLOCK * CAP).astype(jnp.int32) for k in range(LOCAL - 1))
    rest = row - local * (BLOCK * CAP)
    msg = sum((rest >= (k + 1) * CAP).astype(jnp.int32) for k in range(BLOCK - 1))
    slot = rest - msg * CAP
    place = msg * PAIR + local * CAP + slot
    return (lax.broadcasted_iota(jnp.int32, (size, size), 0) == place).astype(jnp.bfloat16)


def dot(a, b):
    return jnp.dot(a, b, preferred_element_type=jnp.float32)


def dot_t(a, b):
    return lax.dot_general(a, b, (((1,), (1,)), ((), ())), preferred_element_type=jnp.float32)


def t_dot(a, b):
    return lax.dot_general(a, b, (((0,), (0,)), ((), ())), preferred_element_type=jnp.float32)


def kernel(
    norm_scale,
    ids_hbm,
    samples_hbm,
    cot_hbm,
    weights_ref,
    grads_ref,
    wgrads_ref,
    ids_ref,
    samples_ref,
    cot_ref,
    into_ref,
    back_ref,
    send_buf,
    recv_buf,
    ysend_buf,
    yrecv_buf,
    x_group,
    g_group,
    y_group,
    act0,
    act1,
    pre0,
    pre1,
    wfull,
    wg_own,
    wg_send,
    wg_recv,
    wg_out,
    g_out,
    target_col,
    acc,
    in_sem,
    send_sem,
    recv_sem,
    ysend_sem,
    yrecv_sem,
    wlocal_sem,
    wsend_sem,
    wrecv_sem,
    gsend_sem,
    grecv_sem,
    out_sem,
    gout_sem,
):
    me = lax.axis_index("expert")
    node = lax.axis_index("node")
    my_x = lax.rem(me, 4)
    my_y = lax.rem(lax.div(me, 4), 4)
    my_z = lax.div(me, 16)

    def shifted(pos, sign):
        dx = lax.rem(pos, 4)
        dy = lax.rem(lax.div(pos, 4), 4)
        dz = lax.rem(lax.div(pos, 16) + dx + dy, 4)
        px = lax.rem(my_x + sign * dx + 4, 4)
        py = lax.rem(my_y + sign * dy + 4, 4)
        pz = lax.rem(my_z + sign * dz + 4, 4)
        return pz * 16 + py * 4 + px

    loads = [
        pltpu.make_async_copy(src, dst, in_sem.at[k])
        for k, (src, dst) in enumerate(
            ((ids_hbm, ids_ref), (samples_hbm, samples_ref), (cot_hbm, cot_ref))
        )
    ]
    for load in loads:
        load.start()
    barrier = pltpu.get_barrier_semaphore()

    for step in range(1, PEERS):
        peer = 16 * ((my_z + step // 16) & 3) + 4 * ((my_y + step // 4 % 4) & 3)
        peer = peer + ((my_x + step % 4) & 3)
        pl.semaphore_signal(barrier, inc=1, device_id=(peer, node), device_id_type=MESH)
    pl.semaphore_signal(barrier, inc=1, device_id=(me, 1 - node), device_id_type=MESH)

    my_half = pl.ds(pl.multiple_of(node * HALF, HALF), HALF)
    w_local = pltpu.make_async_copy(weights_ref, wfull.at[:, :, my_half, :], wlocal_sem)
    w_local.start()
    w_remote = pltpu.make_async_remote_copy(
        src_ref=weights_ref,
        dst_ref=wfull.at[:, :, my_half, :],
        send_sem=wsend_sem,
        recv_sem=wrecv_sem,
        device_id=(me, 1 - node),
        device_id_type=MESH,
    )

    loads[0].wait()
    ids = ids_ref[...]
    onehot = lax.broadcasted_iota(jnp.int32, (EXPERTS, ROWS), 0) == ids
    before = lax.broadcasted_iota(jnp.int32, (ROWS, ROWS), 0) < lax.broadcasted_iota(
        jnp.int32, (ROWS, ROWS), 1
    )
    earlier = dot(onehot.astype(jnp.bfloat16), before.astype(jnp.bfloat16))
    slot = jnp.sum(jnp.where(onehot, earlier, 0.0), axis=0, keepdims=True).astype(jnp.int32)
    owner = ids >> 2
    dx = ((owner & 3) - my_x + 4) & 3
    dy = (((owner >> 2) & 3) - my_y + 4) & 3
    dz = ((owner >> 4) - my_z + 4) & 3
    pos_of = ((dz - dx - dy + 8) & 3) * 16 + dy * 4 + dx
    target = pos_of * PAIR + (ids & 3) * CAP + slot

    def message(pos):
        return pltpu.make_async_remote_copy(
            src_ref=send_buf.at[pos],
            dst_ref=recv_buf.at[pos],
            send_sem=send_sem.at[pos],
            recv_sem=recv_sem.at[pos],
            device_id=(shifted(pos, 1), node),
            device_id_type=MESH,
        )

    def reply(pos):
        return pltpu.make_async_remote_copy(
            src_ref=ysend_buf.at[pos],
            dst_ref=yrecv_buf.at[pos],
            send_sem=ysend_sem.at[pos],
            recv_sem=yrecv_sem.at[pos],
            device_id=(shifted(pos, -1), node),
            device_id_type=MESH,
        )

    def over(low, high, action):
        def step(pos, carry):
            action(pos)
            return carry

        lax.fori_loop(low, high, step, 0)

    def first_of(group):
        return jnp.where(group == 0, 1, group * GROUP)

    loads[1].wait()
    loads[2].wait()

    def build(group):
        rows = lax.broadcasted_iota(jnp.int32, (GROUP * PAIR, ROWS), 0) + group * (GROUP * PAIR)
        pick = (rows == target).astype(jnp.bfloat16)
        feats = dot(pick, samples_ref[...])
        cots = dot(pick, cot_ref[...])
        for j in range(GROUP):
            part = slice(j * PAIR, (j + 1) * PAIR)
            both = jnp.concatenate([feats[part], cots[part]], 0).astype(jnp.bfloat16)
            send_buf[group * GROUP + j] = both

    build(0)
    recv_buf[0] = send_buf[0]
    pl.semaphore_wait(barrier, PEERS)
    over(1, GROUP, lambda pos: message(pos).start())
    w_remote.start()

    def dispatch(group, carry):
        build(group)
        over(group * GROUP, (group + 1) * GROUP, lambda pos: message(pos).start())
        return carry

    lax.fori_loop(1, GROUPS, dispatch, 0)
    into_ref[...] = sort_matrix()
    back_ref[...] = unsort_matrix()
    target_col[...] = jnp.broadcast_to(target.astype(jnp.float32), (128, ROWS)).T
    w_local.wait()
    w_remote.wait()

    def slope(val, sig):
        return sig * (1.0 + val * (1.0 - sig))

    def compute(group, carry):
        over(first_of(group), (group + 1) * GROUP, lambda pos: message(pos).wait_recv())
        for block in range(BLOCKS):
            start = group * GROUP + block * BLOCK
            received = recv_buf[pl.ds(start, BLOCK)].reshape(BLOCK * MSG, FEAT)
            ordered = dot(into_ref[...], received).astype(jnp.bfloat16)
            size = BLOCK * CAP
            for local in range(LOCAL):
                x_group[local, block * size : (block + 1) * size] = ordered[
                    local * size : (local + 1) * size
                ]
                g_group[local, block * size : (block + 1) * size] = ordered[
                    BLOCK * PAIR + local * size : BLOCK * PAIR + (local + 1) * size
                ]
        rows = pl.ds(pl.multiple_of(group * GROUP_ROWS, GROUP_ROWS), GROUP_ROWS)

        def expert(local, inner):
            feats = x_group[local]
            act0[local, rows] = feats
            val0 = dot(feats, wfull[local, 0])
            sig0 = jax.nn.sigmoid(val0)
            hidden = (val0 * sig0).astype(jnp.bfloat16)
            act1[local, rows] = hidden
            val1 = dot(hidden, wfull[local, 1])
            sig1 = jax.nn.sigmoid(val1)
            grad1 = (g_group[local].astype(jnp.float32) * slope(val1, sig1)).astype(jnp.bfloat16)
            pre1[local, rows] = grad1
            back1 = dot_t(grad1, wfull[local, 1]).astype(jnp.bfloat16).astype(jnp.float32)
            grad0 = (back1 * slope(val0, sig0)).astype(jnp.bfloat16)
            pre0[local, rows] = grad0
            y_group[local] = dot_t(grad0, wfull[local, 0]).astype(jnp.bfloat16)
            return inner

        lax.fori_loop(0, LOCAL, expert, 0)
        for block in range(BLOCKS):
            size = BLOCK * CAP
            by_expert = y_group[:, block * size : (block + 1) * size].reshape(BLOCK * PAIR, FEAT)
            by_message = dot(back_ref[...], by_expert)
            for j in range(BLOCK):
                part = slice(j * PAIR, (j + 1) * PAIR)
                both = jnp.concatenate([by_message[part, :HALF], by_message[part, HALF:]], 0)
                both = both.astype(jnp.bfloat16)
                ysend_buf[group * GROUP + block * BLOCK + j] = both
                if block == 0 and j == 0:

                    @pl.when(group == 0)
                    def _():
                        yrecv_buf[0] = both

        over(first_of(group), (group + 1) * GROUP, lambda pos: reply(pos).start())
        return carry

    lax.fori_loop(0, GROUPS, compute, 0)

    other_half = pl.ds(pl.multiple_of((1 - node) * HALF, HALF), HALF)

    def wg_copy(local):
        return pltpu.make_async_remote_copy(
            src_ref=wg_send.at[local],
            dst_ref=wg_recv.at[local],
            send_sem=gsend_sem.at[local],
            recv_sem=grecv_sem.at[local],
            device_id=(me, 1 - node),
            device_id_type=MESH,
        )

    def weight_grads(local, carry):
        for layer, (act, pre) in enumerate(((act0, pre0), (act1, pre1))):
            grad = pre[local]
            sent = t_dot(act[local, :, other_half], grad) * norm_scale
            wg_send[local, layer] = sent.astype(jnp.bfloat16)
            kept = t_dot(act[local, :, my_half], grad) * norm_scale
            wg_own[local, layer] = kept.astype(jnp.bfloat16)
        wg_copy(local).start()
        return carry

    lax.fori_loop(0, LOCAL, weight_grads, 0)

    def wg_store(local):
        return pltpu.make_async_copy(wg_out.at[local], wgrads_ref.at[local], out_sem.at[local])

    def add_grads(local, carry):
        wg_copy(local).wait()
        total = wg_own[local].astype(jnp.float32) + wg_recv[local].astype(jnp.float32)
        wg_out[local] = total.astype(jnp.bfloat16)
        wg_store(local).start()
        return carry

    lax.fori_loop(0, LOCAL, add_grads, 0)

    acc[...] = jnp.zeros_like(acc)

    def combine(group, carry):
        over(first_of(group), (group + 1) * GROUP, lambda pos: reply(pos).wait_recv())
        received = yrecv_buf[pl.ds(group * GROUP, GROUP)].astype(jnp.float32)
        left = received[:, :PAIR].reshape(GROUP * PAIR, HALF)
        right = received[:, PAIR:].reshape(GROUP * PAIR, HALF)
        ordered = jnp.concatenate([left, right], 1).astype(jnp.bfloat16)
        columns = lax.broadcasted_iota(jnp.int32, (ROWS, GROUP * PAIR), 1) + group * (GROUP * PAIR)
        pick = (target_col[:, :1].astype(jnp.int32) == columns).astype(jnp.bfloat16)
        acc[...] += dot(pick, ordered)
        return carry

    lax.fori_loop(0, GROUPS, combine, 0)
    g_out[...] = acc[...].astype(jnp.bfloat16)
    g_store = pltpu.make_async_copy(g_out, grads_ref, gout_sem)
    g_store.start()
    over(1, PEERS, lambda pos: message(pos).wait_send())
    over(1, PEERS, lambda pos: reply(pos).wait_send())
    over(0, LOCAL, lambda local: wg_store(local).wait())
    g_store.wait()


def hand_over(grads_in, wgrads_in, grads_out, wgrads_out, grads_buf, wgrads_buf, in_sem, out_sem):
    half = ROWS // 2
    parts = [
        (src.at[part], buf.at[part], dst.at[part])
        for src, buf, dst, all_parts in (
            (wgrads_in, wgrads_buf, wgrads_out, range(LOCAL)),
            (grads_in, grads_buf, grads_out, [pl.ds(k * half, half) for k in range(2)]),
        )
        for part in all_parts
    ]
    reads = [pltpu.make_async_copy(p[0], p[1], in_sem.at[k]) for k, p in enumerate(parts)]
    writes = [pltpu.make_async_copy(p[1], p[2], out_sem.at[k]) for k, p in enumerate(parts)]
    for copy in reads:
        copy.start()
    for read, write in zip(reads, writes):
        read.wait()
        write.start()
    for copy in writes:
        copy.wait()


def on_device(samples, cotangent, weights, expert_ids):
    bf16 = jnp.bfloat16
    node_count = lax.axis_size("node")
    norm_scale = 1.0 / math.sqrt(ROWS * node_count / LOCAL)
    hbm = pl.BlockSpec(memory_space=pltpu.HBM)
    outs = (
        jax.ShapeDtypeStruct((ROWS, FEAT), bf16),
        jax.ShapeDtypeStruct((LOCAL, 2, HALF, FEAT), bf16),
    )
    results = pl.pallas_call(
        functools.partial(kernel, norm_scale),
        out_shape=outs,
        in_specs=[hbm] * 4,
        out_specs=(hbm, hbm),
        scratch_shapes=[
            pltpu.VMEM((1, ROWS), jnp.int32),
            pltpu.VMEM((ROWS, FEAT), bf16),
            pltpu.VMEM((ROWS, FEAT), bf16),
            pltpu.VMEM((BLOCK * MSG, BLOCK * MSG), bf16),
            pltpu.VMEM((BLOCK * PAIR, BLOCK * PAIR), bf16),
            pltpu.VMEM((PEERS, MSG, FEAT), bf16),
            pltpu.VMEM((PEERS, MSG, FEAT), bf16),
            pltpu.VMEM((PEERS, MSG, HALF), bf16),
            pltpu.VMEM((PEERS, MSG, HALF), bf16),
            pltpu.VMEM((LOCAL, GROUP_ROWS, FEAT), bf16),
            pltpu.VMEM((LOCAL, GROUP_ROWS, FEAT), bf16),
            pltpu.VMEM((LOCAL, GROUP_ROWS, FEAT), bf16),
            pltpu.VMEM((LOCAL, EXPERT_ROWS, FEAT), bf16),
            pltpu.VMEM((LOCAL, EXPERT_ROWS, FEAT), bf16),
            pltpu.VMEM((LOCAL, EXPERT_ROWS, FEAT), bf16),
            pltpu.VMEM((LOCAL, EXPERT_ROWS, FEAT), bf16),
            pltpu.VMEM((LOCAL, 2, FEAT, FEAT), bf16),
            pltpu.VMEM((LOCAL, 2, HALF, FEAT), bf16),
            pltpu.VMEM((LOCAL, 2, HALF, FEAT), bf16),
            pltpu.VMEM((LOCAL, 2, HALF, FEAT), bf16),
            pltpu.VMEM((LOCAL, 2, HALF, FEAT), bf16),
            pltpu.VMEM((ROWS, FEAT), bf16),
            pltpu.VMEM((ROWS, 128), jnp.float32),
            pltpu.VMEM((ROWS, FEAT), jnp.float32),
            pltpu.SemaphoreType.DMA((3,)),
            pltpu.SemaphoreType.DMA((PEERS,)),
            pltpu.SemaphoreType.DMA((PEERS,)),
            pltpu.SemaphoreType.DMA((PEERS,)),
            pltpu.SemaphoreType.DMA((PEERS,)),
            pltpu.SemaphoreType.DMA,
            pltpu.SemaphoreType.DMA,
            pltpu.SemaphoreType.DMA,
            pltpu.SemaphoreType.DMA((LOCAL,)),
            pltpu.SemaphoreType.DMA((LOCAL,)),
            pltpu.SemaphoreType.DMA((LOCAL,)),
            pltpu.SemaphoreType.DMA,
        ],
        compiler_params=pltpu.CompilerParams(
            collective_id=0, has_side_effects=True, vmem_limit_bytes=60 * 1024 * 1024
        ),
    )(
        expert_ids.reshape(1, ROWS),
        samples,
        cotangent,
        weights,
    )
    return pl.pallas_call(
        hand_over,
        out_shape=outs,
        in_specs=[hbm] * 2,
        out_specs=(hbm, hbm),
        scratch_shapes=[
            pltpu.VMEM((ROWS, FEAT), bf16),
            pltpu.VMEM((LOCAL, 2, HALF, FEAT), bf16),
            pltpu.SemaphoreType.DMA((LOCAL + 2,)),
            pltpu.SemaphoreType.DMA((LOCAL + 2,)),
        ],
        compiler_params=pltpu.CompilerParams(vmem_limit_bytes=60 * 1024 * 1024),
    )(*results)


def solution(mesh):
    return jax.shard_map(
        on_device,
        mesh=mesh,
        in_specs=(
            P(("expert", "node"), None),
            P(("expert", "node"), None),
            P("expert", None, "node", None),
            P(("expert", "node"), None),
        ),
        out_specs=(P(("expert", "node"), None), P("expert", None, "node", None)),
        check_vma=False,
    )
```

```python
import functools
import math

import jax
import jax.numpy as jnp
from jax import lax
from jax.experimental import pallas as pl
from jax.experimental.pallas import tpu as pltpu
from jax.sharding import PartitionSpec as P

MESH = pl.DeviceIdType.MESH
ROWS = 768
FEAT = 512
HALF = 256
EXPERTS = 256
LOCAL = 4
CAP = 6
PAIR = LOCAL * CAP
MSG = 2 * PAIR
PEERS = 64
GROUP = 16
GROUPS = PEERS // GROUP
BLOCK = 4
BLOCKS = GROUP // BLOCK
GROUP_ROWS = GROUP * CAP
EXPERT_ROWS = PEERS * CAP


def sort_matrix():
    size = BLOCK * MSG
    row = lax.broadcasted_iota(jnp.int32, (1, size), 1)
    msg = sum((row >= (k + 1) * MSG).astype(jnp.int32) for k in range(BLOCK - 1))
    rest = row - msg * MSG
    kind = (rest >= PAIR).astype(jnp.int32)
    rest = rest - kind * PAIR
    local = sum((rest >= (k + 1) * CAP).astype(jnp.int32) for k in range(LOCAL - 1))
    slot = rest - local * CAP
    place = kind * (BLOCK * PAIR) + local * (BLOCK * CAP) + msg * CAP + slot
    return (lax.broadcasted_iota(jnp.int32, (size, size), 0) == place).astype(jnp.bfloat16)


def unsort_matrix():
    size = BLOCK * PAIR
    row = lax.broadcasted_iota(jnp.int32, (1, size), 1)
    local = sum((row >= (k + 1) * BLOCK * CAP).astype(jnp.int32) for k in range(LOCAL - 1))
    rest = row - local * (BLOCK * CAP)
    msg = sum((rest >= (k + 1) * CAP).astype(jnp.int32) for k in range(BLOCK - 1))
    slot = rest - msg * CAP
    place = msg * PAIR + local * CAP + slot
    return (lax.broadcasted_iota(jnp.int32, (size, size), 0) == place).astype(jnp.bfloat16)


def dot(a, b):
    return jnp.dot(a, b, preferred_element_type=jnp.float32)


def dot_t(a, b):
    return lax.dot_general(a, b, (((1,), (1,)), ((), ())), preferred_element_type=jnp.float32)


def t_dot(a, b):
    return lax.dot_general(a, b, (((0,), (0,)), ((), ())), preferred_element_type=jnp.float32)


def kernel(
    norm_scale,
    ids_hbm,
    samples_hbm,
    cot_hbm,
    weights_ref,
    grads_ref,
    wgrads_ref,
    ids_ref,
    samples_ref,
    cot_ref,
    into_ref,
    back_ref,
    send_buf,
    recv_buf,
    ysend_buf,
    yrecv_buf,
    g_group,
    slope0,
    act0,
    act1,
    pre0,
    pre1,
    wfull,
    wg_acc,
    wg_own,
    wg_send,
    wg_recv,
    wg_out,
    g_out,
    target_col,
    acc,
    in_sem,
    send_sem,
    recv_sem,
    ysend_sem,
    yrecv_sem,
    wlocal_sem,
    wsend_sem,
    wrecv_sem,
    gsend_sem,
    grecv_sem,
    out_sem,
    gout_sem,
):
    me = lax.axis_index("expert")
    node = lax.axis_index("node")
    my_x = lax.rem(me, 4)
    my_y = lax.rem(lax.div(me, 4), 4)
    my_z = lax.div(me, 16)

    def shifted(pos, sign):
        dx = lax.rem(pos, 4)
        dy = lax.rem(lax.div(pos, 4), 4)
        dz = lax.rem(lax.div(pos, 16) + dx + dy, 4)
        px = lax.rem(my_x + sign * dx + 4, 4)
        py = lax.rem(my_y + sign * dy + 4, 4)
        pz = lax.rem(my_z + sign * dz + 4, 4)
        return pz * 16 + py * 4 + px

    loads = [
        pltpu.make_async_copy(src, dst, in_sem.at[k])
        for k, (src, dst) in enumerate(
            ((ids_hbm, ids_ref), (samples_hbm, samples_ref), (cot_hbm, cot_ref))
        )
    ]
    for load in loads:
        load.start()
    barrier = pltpu.get_barrier_semaphore()

    for step in range(1, PEERS):
        peer = 16 * ((my_z + step // 16) & 3) + 4 * ((my_y + step // 4 % 4) & 3)
        peer = peer + ((my_x + step % 4) & 3)
        pl.semaphore_signal(barrier, inc=1, device_id=(peer, node), device_id_type=MESH)
    pl.semaphore_signal(barrier, inc=1, device_id=(me, 1 - node), device_id_type=MESH)

    my_half = pl.ds(pl.multiple_of(node * HALF, HALF), HALF)
    w_local = pltpu.make_async_copy(weights_ref, wfull.at[:, :, my_half, :], wlocal_sem)
    w_local.start()
    w_remote = pltpu.make_async_remote_copy(
        src_ref=weights_ref,
        dst_ref=wfull.at[:, :, my_half, :],
        send_sem=wsend_sem,
        recv_sem=wrecv_sem,
        device_id=(me, 1 - node),
        device_id_type=MESH,
    )

    loads[0].wait()
    ids = ids_ref[...]
    onehot = lax.broadcasted_iota(jnp.int32, (EXPERTS, ROWS), 0) == ids
    before = lax.broadcasted_iota(jnp.int32, (ROWS, ROWS), 0) < lax.broadcasted_iota(
        jnp.int32, (ROWS, ROWS), 1
    )
    earlier = dot(onehot.astype(jnp.bfloat16), before.astype(jnp.bfloat16))
    slot = jnp.sum(jnp.where(onehot, earlier, 0.0), axis=0, keepdims=True).astype(jnp.int32)
    owner = ids >> 2
    dx = ((owner & 3) - my_x + 4) & 3
    dy = (((owner >> 2) & 3) - my_y + 4) & 3
    dz = ((owner >> 4) - my_z + 4) & 3
    pos_of = ((dz - dx - dy + 8) & 3) * 16 + dy * 4 + dx
    target = pos_of * PAIR + (ids & 3) * CAP + slot

    def message(pos):
        return pltpu.make_async_remote_copy(
            src_ref=send_buf.at[pos],
            dst_ref=recv_buf.at[pos],
            send_sem=send_sem.at[pos],
            recv_sem=recv_sem.at[pos],
            device_id=(shifted(pos, 1), node),
            device_id_type=MESH,
        )

    def reply(pos):
        return pltpu.make_async_remote_copy(
            src_ref=ysend_buf.at[pos],
            dst_ref=yrecv_buf.at[pos],
            send_sem=ysend_sem.at[pos],
            recv_sem=yrecv_sem.at[pos],
            device_id=(shifted(pos, -1), node),
            device_id_type=MESH,
        )

    def over(low, high, action):
        def step(pos, carry):
            action(pos)
            return carry

        lax.fori_loop(low, high, step, 0)

    def first_of(group):
        return jnp.where(group == 0, 1, group * GROUP)

    loads[1].wait()
    loads[2].wait()

    def build(group):
        rows = lax.broadcasted_iota(jnp.int32, (GROUP * PAIR, ROWS), 0) + group * (GROUP * PAIR)
        pick = (rows == target).astype(jnp.bfloat16)
        feats = dot(pick, samples_ref[...])
        cots = dot(pick, cot_ref[...])
        for j in range(GROUP):
            part = slice(j * PAIR, (j + 1) * PAIR)
            both = jnp.concatenate([feats[part], cots[part]], 0).astype(jnp.bfloat16)
            send_buf[group * GROUP + j] = both

    build(0)
    recv_buf[0] = send_buf[0]
    pl.semaphore_wait(barrier, PEERS)
    over(1, GROUP, lambda pos: message(pos).start())
    w_remote.start()

    def dispatch(group, carry):
        build(group)
        over(group * GROUP, (group + 1) * GROUP, lambda pos: message(pos).start())
        return carry

    lax.fori_loop(1, GROUPS, dispatch, 0)
    into_ref[...] = sort_matrix()
    back_ref[...] = unsort_matrix()
    target_col[...] = jnp.broadcast_to(target.astype(jnp.float32), (128, ROWS)).T
    w_local.wait()
    w_remote.wait()

    def slope(val, sig):
        return sig * (1.0 + val * (1.0 - sig))

    def compute(group, carry):
        over(first_of(group), (group + 1) * GROUP, lambda pos: message(pos).wait_recv())
        size = BLOCK * CAP
        ordered = []
        for block in range(BLOCKS):
            received = recv_buf[pl.ds(group * GROUP + block * BLOCK, BLOCK)]
            ordered.append(dot(into_ref[...], received.reshape(BLOCK * MSG, FEAT)))

        def rows_of(place):
            return jnp.concatenate([part[place * size : (place + 1) * size] for part in ordered], 0)

        rows = pl.ds(pl.multiple_of(group * GROUP_ROWS, GROUP_ROWS), GROUP_ROWS)
        experts = range(LOCAL)
        for e in experts:
            act0[e, rows] = rows_of(e).astype(jnp.bfloat16)
            g_group[e] = rows_of(LOCAL + e)
        val0 = [dot(act0[e, rows], wfull[e, 0]) for e in experts]
        for e in experts:
            sig = jax.nn.sigmoid(val0[e])
            act1[e, rows] = (val0[e] * sig).astype(jnp.bfloat16)
            slope0[e] = slope(val0[e], sig)
        val1 = [dot(act1[e, rows], wfull[e, 1]) for e in experts]
        for e in experts:
            sig = jax.nn.sigmoid(val1[e])
            pre1[e, rows] = (g_group[e] * slope(val1[e], sig)).astype(jnp.bfloat16)
        back1 = [dot_t(pre1[e, rows], wfull[e, 1]) for e in experts]
        for e in experts:
            grad = back1[e].astype(jnp.bfloat16).astype(jnp.float32)
            pre0[e, rows] = (grad * slope0[e]).astype(jnp.bfloat16)
        back0 = [dot_t(pre0[e, rows], wfull[e, 0]) for e in experts]
        for block in range(BLOCKS):
            part = slice(block * size, (block + 1) * size)
            by_expert = jnp.concatenate([back0[e][part] for e in experts], 0).astype(jnp.bfloat16)
            by_message = dot(back_ref[...], by_expert)
            for j in range(BLOCK):
                part = slice(j * PAIR, (j + 1) * PAIR)
                both = jnp.concatenate([by_message[part, :HALF], by_message[part, HALF:]], 0)
                ysend_buf[group * GROUP + block * BLOCK + j] = both.astype(jnp.bfloat16)

        over(first_of(group), (group + 1) * GROUP, lambda pos: reply(pos).start())
        return carry

    other_half = pl.ds(pl.multiple_of((1 - node) * HALF, HALF), HALF)

    def wg_copy(local):
        return pltpu.make_async_remote_copy(
            src_ref=wg_send.at[local],
            dst_ref=wg_recv.at[local],
            send_sem=gsend_sem.at[local],
            recv_sem=grecv_sem.at[local],
            device_id=(me, 1 - node),
            device_id_type=MESH,
        )

    layers = ((act0, pre0), (act1, pre1))
    span = EXPERT_ROWS // 2

    def first_grads(local, carry):
        for layer, (act, pre) in enumerate(layers):
            wg_acc[local, layer] = t_dot(act[local, :span], pre[local, :span])
        return carry

    def last_grads(local, carry):
        for layer, (act, pre) in enumerate(layers):
            for half, result in ((other_half, wg_send), (my_half, wg_own)):
                total = wg_acc[local, layer, half] + t_dot(
                    act[local, span:, half], pre[local, span:]
                )
                result[local, layer] = (total * norm_scale).astype(jnp.bfloat16)
        wg_copy(local).start()
        return carry

    def wg_store(local):
        return pltpu.make_async_copy(wg_out.at[local], wgrads_ref.at[local], out_sem.at[local])

    def add_grads(local, carry):
        wg_copy(local).wait()
        total = wg_own[local].astype(jnp.float32) + wg_recv[local].astype(jnp.float32)
        wg_out[local] = total.astype(jnp.bfloat16)
        wg_store(local).start()
        return carry

    lax.fori_loop(0, 2, compute, 0)
    lax.fori_loop(0, LOCAL, first_grads, 0)
    lax.fori_loop(2, GROUPS, compute, 0)
    lax.fori_loop(0, LOCAL, last_grads, 0)
    yrecv_buf[0] = ysend_buf[0]

    acc[...] = jnp.zeros_like(acc)

    def combine(group, carry):
        over(first_of(group), (group + 1) * GROUP, lambda pos: reply(pos).wait_recv())
        received = yrecv_buf[pl.ds(group * GROUP, GROUP)].astype(jnp.float32)
        left = received[:, :PAIR].reshape(GROUP * PAIR, HALF)
        right = received[:, PAIR:].reshape(GROUP * PAIR, HALF)
        ordered = jnp.concatenate([left, right], 1).astype(jnp.bfloat16)
        columns = lax.broadcasted_iota(jnp.int32, (ROWS, GROUP * PAIR), 1) + group * (GROUP * PAIR)
        pick = (target_col[:, :1].astype(jnp.int32) == columns).astype(jnp.bfloat16)
        acc[...] += dot(pick, ordered)
        return carry

    lax.fori_loop(0, GROUPS - 1, combine, 0)
    lax.fori_loop(0, LOCAL, add_grads, 0)
    combine(GROUPS - 1, 0)
    g_out[...] = acc[...].astype(jnp.bfloat16)
    g_store = pltpu.make_async_copy(g_out, grads_ref, gout_sem)
    g_store.start()
    over(1, PEERS, lambda pos: message(pos).wait_send())
    over(1, PEERS, lambda pos: reply(pos).wait_send())
    over(0, LOCAL, lambda local: wg_store(local).wait())
    g_store.wait()


def hand_over(grads_in, wgrads_in, grads_out, wgrads_out, grads_buf, wgrads_buf, in_sem, out_sem):
    half = ROWS // 2
    parts = [
        (src.at[part], buf.at[part], dst.at[part])
        for src, buf, dst, all_parts in (
            (wgrads_in, wgrads_buf, wgrads_out, range(LOCAL)),
            (grads_in, grads_buf, grads_out, [pl.ds(k * half, half) for k in range(2)]),
        )
        for part in all_parts
    ]
    reads = [pltpu.make_async_copy(p[0], p[1], in_sem.at[k]) for k, p in enumerate(parts)]
    writes = [pltpu.make_async_copy(p[1], p[2], out_sem.at[k]) for k, p in enumerate(parts)]
    for copy in reads:
        copy.start()
    for read, write in zip(reads, writes):
        read.wait()
        write.start()
    for copy in writes:
        copy.wait()


def on_device(samples, cotangent, weights, expert_ids):
    bf16 = jnp.bfloat16
    node_count = lax.axis_size("node")
    norm_scale = 1.0 / math.sqrt(ROWS * node_count / LOCAL)
    hbm = pl.BlockSpec(memory_space=pltpu.HBM)
    outs = (
        jax.ShapeDtypeStruct((ROWS, FEAT), bf16),
        jax.ShapeDtypeStruct((LOCAL, 2, HALF, FEAT), bf16),
    )
    results = pl.pallas_call(
        functools.partial(kernel, norm_scale),
        out_shape=outs,
        in_specs=[hbm] * 4,
        out_specs=(hbm, hbm),
        scratch_shapes=[
            pltpu.VMEM((1, ROWS), jnp.int32),
            pltpu.VMEM((ROWS, FEAT), bf16),
            pltpu.VMEM((ROWS, FEAT), bf16),
            pltpu.VMEM((BLOCK * MSG, BLOCK * MSG), bf16),
            pltpu.VMEM((BLOCK * PAIR, BLOCK * PAIR), bf16),
            pltpu.VMEM((PEERS, MSG, FEAT), bf16),
            pltpu.VMEM((PEERS, MSG, FEAT), bf16),
            pltpu.VMEM((PEERS, MSG, HALF), bf16),
            pltpu.VMEM((PEERS, MSG, HALF), bf16),
            pltpu.VMEM((LOCAL, GROUP_ROWS, FEAT), jnp.float32),
            pltpu.VMEM((LOCAL, GROUP_ROWS, FEAT), jnp.float32),
            pltpu.VMEM((LOCAL, EXPERT_ROWS, FEAT), bf16),
            pltpu.VMEM((LOCAL, EXPERT_ROWS, FEAT), bf16),
            pltpu.VMEM((LOCAL, EXPERT_ROWS, FEAT), bf16),
            pltpu.VMEM((LOCAL, EXPERT_ROWS, FEAT), bf16),
            pltpu.VMEM((LOCAL, 2, FEAT, FEAT), bf16),
            pltpu.VMEM((LOCAL, 2, FEAT, FEAT), jnp.float32),
            pltpu.VMEM((LOCAL, 2, HALF, FEAT), bf16),
            pltpu.VMEM((LOCAL, 2, HALF, FEAT), bf16),
            pltpu.VMEM((LOCAL, 2, HALF, FEAT), bf16),
            pltpu.VMEM((LOCAL, 2, HALF, FEAT), bf16),
            pltpu.VMEM((ROWS, FEAT), bf16),
            pltpu.VMEM((ROWS, 128), jnp.float32),
            pltpu.VMEM((ROWS, FEAT), jnp.float32),
            pltpu.SemaphoreType.DMA((3,)),
            pltpu.SemaphoreType.DMA((PEERS,)),
            pltpu.SemaphoreType.DMA((PEERS,)),
            pltpu.SemaphoreType.DMA((PEERS,)),
            pltpu.SemaphoreType.DMA((PEERS,)),
            pltpu.SemaphoreType.DMA,
            pltpu.SemaphoreType.DMA,
            pltpu.SemaphoreType.DMA,
            pltpu.SemaphoreType.DMA((LOCAL,)),
            pltpu.SemaphoreType.DMA((LOCAL,)),
            pltpu.SemaphoreType.DMA((LOCAL,)),
            pltpu.SemaphoreType.DMA,
        ],
        compiler_params=pltpu.CompilerParams(
            collective_id=0, has_side_effects=True, vmem_limit_bytes=60 * 1024 * 1024
        ),
    )(
        expert_ids.reshape(1, ROWS),
        samples,
        cotangent,
        weights,
    )
    return pl.pallas_call(
        hand_over,
        out_shape=outs,
        in_specs=[hbm] * 2,
        out_specs=(hbm, hbm),
        scratch_shapes=[
            pltpu.VMEM((ROWS, FEAT), bf16),
            pltpu.VMEM((LOCAL, 2, HALF, FEAT), bf16),
            pltpu.SemaphoreType.DMA((LOCAL + 2,)),
            pltpu.SemaphoreType.DMA((LOCAL + 2,)),
        ],
        compiler_params=pltpu.CompilerParams(vmem_limit_bytes=60 * 1024 * 1024),
    )(*results)


def solution(mesh):
    return jax.shard_map(
        on_device,
        mesh=mesh,
        in_specs=(
            P(("expert", "node"), None),
            P(("expert", "node"), None),
            P("expert", None, "node", None),
            P(("expert", "node"), None),
        ),
        out_specs=(P(("expert", "node"), None), P("expert", None, "node", None)),
        check_vma=False,
    )
```

```python
import functools
import math

import jax
import jax.numpy as jnp
from jax import lax
from jax.experimental import pallas as pl
from jax.experimental.pallas import tpu as pltpu
from jax.sharding import PartitionSpec as P

MESH = pl.DeviceIdType.MESH
ROWS = 768
FEAT = 512
HALF = 256
EXPERTS = 256
LOCAL = 4
CAP = 6
PAIR = LOCAL * CAP
MSG = 2 * PAIR
PEERS = 64
GROUP = 16
GROUPS = PEERS // GROUP
BLOCK = 4
PASS = 16
GROUP_ROWS = GROUP * CAP
GRAD_PARTS = 4
EXPERT_ROWS = PEERS * CAP


def sort_matrix():
    size = BLOCK * MSG
    row = lax.broadcasted_iota(jnp.int32, (1, size), 1)
    msg = sum((row >= (k + 1) * MSG).astype(jnp.int32) for k in range(BLOCK - 1))
    rest = row - msg * MSG
    kind = (rest >= PAIR).astype(jnp.int32)
    rest = rest - kind * PAIR
    local = sum((rest >= (k + 1) * CAP).astype(jnp.int32) for k in range(LOCAL - 1))
    slot = rest - local * CAP
    place = kind * (BLOCK * PAIR) + local * (BLOCK * CAP) + msg * CAP + slot
    return (lax.broadcasted_iota(jnp.int32, (size, size), 0) == place).astype(jnp.bfloat16)


def unsort_matrix():
    size = BLOCK * PAIR
    row = lax.broadcasted_iota(jnp.int32, (1, size), 1)
    local = sum((row >= (k + 1) * BLOCK * CAP).astype(jnp.int32) for k in range(LOCAL - 1))
    rest = row - local * (BLOCK * CAP)
    msg = sum((rest >= (k + 1) * CAP).astype(jnp.int32) for k in range(BLOCK - 1))
    slot = rest - msg * CAP
    place = msg * PAIR + local * CAP + slot
    return (lax.broadcasted_iota(jnp.int32, (size, size), 0) == place).astype(jnp.bfloat16)


def dot(a, b):
    return jnp.dot(a, b, preferred_element_type=jnp.float32)


def dot_t(a, b):
    return lax.dot_general(a, b, (((1,), (1,)), ((), ())), preferred_element_type=jnp.float32)


def t_dot(a, b):
    return lax.dot_general(a, b, (((0,), (0,)), ((), ())), preferred_element_type=jnp.float32)


def kernel(
    norm_scale,
    ids_hbm,
    samples_hbm,
    cot_hbm,
    weights_ref,
    grads_ref,
    wgrads_ref,
    ids_ref,
    samples_ref,
    cot_ref,
    into_ref,
    back_ref,
    send_buf,
    recv_buf,
    ysend_buf,
    yrecv_buf,
    g_group,
    slope0,
    act0,
    act1,
    pre0,
    pre1,
    wfull,
    wg_acc,
    wg_own,
    wg_send,
    wg_recv,
    wg_out,
    g_out,
    target_col,
    acc,
    in_sem,
    send_sem,
    recv_sem,
    ysend_sem,
    yrecv_sem,
    wlocal_sem,
    wsend_sem,
    wrecv_sem,
    gsend_sem,
    grecv_sem,
    out_sem,
    gout_sem,
):
    me = lax.axis_index("expert")
    node = lax.axis_index("node")
    my_x = lax.rem(me, 4)
    my_y = lax.rem(lax.div(me, 4), 4)
    my_z = lax.div(me, 16)

    def shifted(pos, sign):
        dx = lax.rem(pos, 4)
        dy = lax.rem(lax.div(pos, 4), 4)
        dz = lax.rem(lax.div(pos, 16) + dx + dy, 4)
        px = lax.rem(my_x + sign * dx + 4, 4)
        py = lax.rem(my_y + sign * dy + 4, 4)
        pz = lax.rem(my_z + sign * dz + 4, 4)
        return pz * 16 + py * 4 + px

    loads = [
        pltpu.make_async_copy(src, dst, in_sem.at[k])
        for k, (src, dst) in enumerate(
            ((ids_hbm, ids_ref), (samples_hbm, samples_ref), (cot_hbm, cot_ref))
        )
    ]
    for load in loads:
        load.start()
    barrier = pltpu.get_barrier_semaphore()

    for step in range(1, PEERS):
        peer = 16 * ((my_z + step // 16) & 3) + 4 * ((my_y + step // 4 % 4) & 3)
        peer = peer + ((my_x + step % 4) & 3)
        pl.semaphore_signal(barrier, inc=1, device_id=(peer, node), device_id_type=MESH)
    pl.semaphore_signal(barrier, inc=1, device_id=(me, 1 - node), device_id_type=MESH)

    my_half = pl.ds(pl.multiple_of(node * HALF, HALF), HALF)
    w_local = pltpu.make_async_copy(weights_ref, wfull.at[:, :, my_half, :], wlocal_sem)
    w_local.start()
    w_remote = pltpu.make_async_remote_copy(
        src_ref=weights_ref,
        dst_ref=wfull.at[:, :, my_half, :],
        send_sem=wsend_sem,
        recv_sem=wrecv_sem,
        device_id=(me, 1 - node),
        device_id_type=MESH,
    )

    loads[0].wait()
    ids = ids_ref[...]
    onehot = lax.broadcasted_iota(jnp.int32, (EXPERTS, ROWS), 0) == ids
    before = lax.broadcasted_iota(jnp.int32, (ROWS, ROWS), 0) < lax.broadcasted_iota(
        jnp.int32, (ROWS, ROWS), 1
    )
    earlier = dot(onehot.astype(jnp.bfloat16), before.astype(jnp.bfloat16))
    slot = jnp.sum(jnp.where(onehot, earlier, 0.0), axis=0, keepdims=True).astype(jnp.int32)
    owner = ids >> 2
    dx = ((owner & 3) - my_x + 4) & 3
    dy = (((owner >> 2) & 3) - my_y + 4) & 3
    dz = ((owner >> 4) - my_z + 4) & 3
    pos_of = ((dz - dx - dy + 8) & 3) * 16 + dy * 4 + dx
    target = pos_of * PAIR + (ids & 3) * CAP + slot

    def message(pos):
        return pltpu.make_async_remote_copy(
            src_ref=send_buf.at[pos],
            dst_ref=recv_buf.at[pos],
            send_sem=send_sem.at[pos],
            recv_sem=recv_sem.at[pos],
            device_id=(shifted(pos, 1), node),
            device_id_type=MESH,
        )

    def reply(pos):
        return pltpu.make_async_remote_copy(
            src_ref=ysend_buf.at[pos],
            dst_ref=yrecv_buf.at[pos],
            send_sem=ysend_sem.at[pos],
            recv_sem=yrecv_sem.at[pos],
            device_id=(shifted(pos, -1), node),
            device_id_type=MESH,
        )

    def over(low, high, action):
        def step(pos, carry):
            action(pos)
            return carry

        lax.fori_loop(low, high, step, 0)

    def send_all(copy, first, stride):
        def send(j):
            pos = first + lax.rem(j * stride, GROUP)

            @pl.when(pos != 0)
            def _():
                copy(pos).start()

        over(0, GROUP, send)

    def first_of(group):
        return jnp.where(group == 0, 1, group * GROUP)

    loads[1].wait()
    loads[2].wait()

    def build(group):
        rows = lax.broadcasted_iota(jnp.int32, (GROUP * PAIR, ROWS), 0) + group * (GROUP * PAIR)
        pick = (rows == target).astype(jnp.bfloat16)
        feats = dot(pick, samples_ref[...])
        cots = dot(pick, cot_ref[...])
        for j in range(GROUP):
            part = slice(j * PAIR, (j + 1) * PAIR)
            both = jnp.concatenate([feats[part], cots[part]], 0).astype(jnp.bfloat16)
            send_buf[group * GROUP + j] = both

    build(0)
    recv_buf[0] = send_buf[0]
    pl.semaphore_wait(barrier, PEERS)
    send_all(message, 0, 5)
    w_remote.start()

    def dispatch(group, carry):
        build(group)
        send_all(message, group * GROUP, 5)
        return carry

    lax.fori_loop(1, GROUPS, dispatch, 0)
    into_ref[...] = sort_matrix()
    back_ref[...] = unsort_matrix()
    target_col[...] = jnp.broadcast_to(target.astype(jnp.float32), (128, ROWS)).T
    w_local.wait()
    w_remote.wait()

    def slope(val, sig):
        return sig * (1.0 + val * (1.0 - sig))

    def compute(count, first):
        low = jnp.where(first == 0, 1, first)
        over(low, first + count, lambda pos: message(pos).wait_recv())
        size = BLOCK * CAP
        ordered = []
        for block in range(count // BLOCK):
            received = recv_buf[pl.ds(first + block * BLOCK, BLOCK)]
            ordered.append(dot(into_ref[...], received.reshape(BLOCK * MSG, FEAT)))

        def rows_of(place):
            return jnp.concatenate([part[place * size : (place + 1) * size] for part in ordered], 0)

        rows = pl.ds(pl.multiple_of(first * CAP, 16), count * CAP)
        kept = slice(0, count * CAP)
        experts = range(LOCAL)
        for e in experts:
            act0[e, rows] = rows_of(e).astype(jnp.bfloat16)
            g_group[e, kept] = rows_of(LOCAL + e)
        val0 = [dot(act0[e, rows], wfull[e, 0]) for e in experts]
        for e in experts:
            sig = jax.nn.sigmoid(val0[e])
            act1[e, rows] = (val0[e] * sig).astype(jnp.bfloat16)
            slope0[e, kept] = slope(val0[e], sig)
        val1 = [dot(act1[e, rows], wfull[e, 1]) for e in experts]
        for e in experts:
            sig = jax.nn.sigmoid(val1[e])
            pre1[e, rows] = (g_group[e, kept] * slope(val1[e], sig)).astype(jnp.bfloat16)
        back1 = [dot_t(pre1[e, rows], wfull[e, 1]) for e in experts]
        for e in experts:
            grad = back1[e].astype(jnp.bfloat16).astype(jnp.float32)
            pre0[e, rows] = (grad * slope0[e, kept]).astype(jnp.bfloat16)
        back0 = [dot_t(pre0[e, rows], wfull[e, 0]) for e in experts]
        for block in range(count // BLOCK):
            part = slice(block * size, (block + 1) * size)
            by_expert = jnp.concatenate([back0[e][part] for e in experts], 0).astype(jnp.bfloat16)
            by_message = dot(back_ref[...], by_expert)
            for j in range(BLOCK):
                part = slice(j * PAIR, (j + 1) * PAIR)
                both = jnp.concatenate([by_message[part, :HALF], by_message[part, HALF:]], 0)
                ysend_buf[first + block * BLOCK + j] = both.astype(jnp.bfloat16)

        send_all(reply, first, 13)

    other_half = pl.ds(pl.multiple_of((1 - node) * HALF, HALF), HALF)

    def wg_copy(local):
        return pltpu.make_async_remote_copy(
            src_ref=wg_send.at[local],
            dst_ref=wg_recv.at[local],
            send_sem=gsend_sem.at[local],
            recv_sem=grecv_sem.at[local],
            device_id=(me, 1 - node),
            device_id_type=MESH,
        )

    layers = ((act0, pre0), (act1, pre1))
    span = EXPERT_ROWS // 2

    def first_grads(local, carry):
        for layer, (act, pre) in enumerate(layers):
            wg_acc[local, layer] = t_dot(act[local, :span], pre[local, :span])
        return carry

    def last_grads(local, carry):
        for layer, (act, pre) in enumerate(layers):
            for half, result in ((other_half, wg_send), (my_half, wg_own)):
                total = wg_acc[local, layer, half] + t_dot(
                    act[local, span:, half], pre[local, span:]
                )
                result[local, layer] = (total * norm_scale).astype(jnp.bfloat16)
        wg_copy(local).start()
        return carry

    def wg_store(local):
        return pltpu.make_async_copy(wg_out.at[local], wgrads_ref.at[local], out_sem.at[local])

    def add_grads(local, carry):
        wg_copy(local).wait()
        total = wg_own[local].astype(jnp.float32) + wg_recv[local].astype(jnp.float32)
        wg_out[local] = total.astype(jnp.bfloat16)
        wg_store(local).start()
        return carry

    def pass_of(step):
        compute(PASS, step * PASS)

        @pl.when(step == PEERS // PASS // 2 - 1)
        def _():
            lax.fori_loop(0, LOCAL, first_grads, 0)

    over(0, PEERS // PASS, pass_of)
    lax.fori_loop(0, LOCAL, last_grads, 0)
    yrecv_buf[0] = ysend_buf[0]

    acc[...] = jnp.zeros_like(acc)

    def combine(group, carry):
        over(first_of(group), (group + 1) * GROUP, lambda pos: reply(pos).wait_recv())
        received = yrecv_buf[pl.ds(group * GROUP, GROUP)].astype(jnp.float32)
        left = received[:, :PAIR].reshape(GROUP * PAIR, HALF)
        right = received[:, PAIR:].reshape(GROUP * PAIR, HALF)
        ordered = jnp.concatenate([left, right], 1).astype(jnp.bfloat16)
        columns = lax.broadcasted_iota(jnp.int32, (ROWS, GROUP * PAIR), 1) + group * (GROUP * PAIR)
        pick = (target_col[:, :1].astype(jnp.int32) == columns).astype(jnp.bfloat16)
        acc[...] += dot(pick, ordered)
        return carry

    lax.fori_loop(0, GROUPS - 1, combine, 0)
    lax.fori_loop(0, LOCAL, add_grads, 0)
    combine(GROUPS - 1, 0)
    g_out[...] = acc[...].astype(jnp.bfloat16)
    g_store = pltpu.make_async_copy(g_out, grads_ref, gout_sem)
    g_store.start()
    over(1, PEERS, lambda pos: message(pos).wait_send())
    over(1, PEERS, lambda pos: reply(pos).wait_send())
    over(0, LOCAL, lambda local: wg_store(local).wait())
    g_store.wait()


def hand_over(grads_in, wgrads_in, grads_out, wgrads_out, grads_buf, wgrads_buf, in_sem, out_sem):
    size = ROWS // GRAD_PARTS
    rows = [pl.ds(k * size, size) for k in range(GRAD_PARTS)]
    parts = [
        (src.at[part], buf.at[part], dst.at[part])
        for src, buf, dst, all_parts in (
            (wgrads_in, wgrads_buf, wgrads_out, [(k, j) for k in range(LOCAL) for j in range(2)]),
            (grads_in, grads_buf, grads_out, rows),
        )
        for part in all_parts
    ]
    reads = [pltpu.make_async_copy(p[0], p[1], in_sem.at[k]) for k, p in enumerate(parts)]
    writes = [pltpu.make_async_copy(p[1], p[2], out_sem.at[k]) for k, p in enumerate(parts)]
    for copy in reads:
        copy.start()
    for read, write in zip(reads, writes):
        read.wait()
        write.start()
    for copy in writes:
        copy.wait()


def on_device(samples, cotangent, weights, expert_ids):
    bf16 = jnp.bfloat16
    node_count = lax.axis_size("node")
    norm_scale = 1.0 / math.sqrt(ROWS * node_count / LOCAL)
    hbm = pl.BlockSpec(memory_space=pltpu.HBM)
    outs = (
        jax.ShapeDtypeStruct((ROWS, FEAT), bf16),
        jax.ShapeDtypeStruct((LOCAL, 2, HALF, FEAT), bf16),
    )
    results = pl.pallas_call(
        functools.partial(kernel, norm_scale),
        out_shape=outs,
        in_specs=[hbm] * 4,
        out_specs=(hbm, hbm),
        scratch_shapes=[
            pltpu.VMEM((1, ROWS), jnp.int32),
            pltpu.VMEM((ROWS, FEAT), bf16),
            pltpu.VMEM((ROWS, FEAT), bf16),
            pltpu.VMEM((BLOCK * MSG, BLOCK * MSG), bf16),
            pltpu.VMEM((BLOCK * PAIR, BLOCK * PAIR), bf16),
            pltpu.VMEM((PEERS, MSG, FEAT), bf16),
            pltpu.VMEM((PEERS, MSG, FEAT), bf16),
            pltpu.VMEM((PEERS, MSG, HALF), bf16),
            pltpu.VMEM((PEERS, MSG, HALF), bf16),
            pltpu.VMEM((LOCAL, GROUP_ROWS, FEAT), jnp.float32),
            pltpu.VMEM((LOCAL, GROUP_ROWS, FEAT), jnp.float32),
            pltpu.VMEM((LOCAL, EXPERT_ROWS, FEAT), bf16),
            pltpu.VMEM((LOCAL, EXPERT_ROWS, FEAT), bf16),
            pltpu.VMEM((LOCAL, EXPERT_ROWS, FEAT), bf16),
            pltpu.VMEM((LOCAL, EXPERT_ROWS, FEAT), bf16),
            pltpu.VMEM((LOCAL, 2, FEAT, FEAT), bf16),
            pltpu.VMEM((LOCAL, 2, FEAT, FEAT), jnp.float32),
            pltpu.VMEM((LOCAL, 2, HALF, FEAT), bf16),
            pltpu.VMEM((LOCAL, 2, HALF, FEAT), bf16),
            pltpu.VMEM((LOCAL, 2, HALF, FEAT), bf16),
            pltpu.VMEM((LOCAL, 2, HALF, FEAT), bf16),
            pltpu.VMEM((ROWS, FEAT), bf16),
            pltpu.VMEM((ROWS, 128), jnp.float32),
            pltpu.VMEM((ROWS, FEAT), jnp.float32),
            pltpu.SemaphoreType.DMA((3,)),
            pltpu.SemaphoreType.DMA((PEERS,)),
            pltpu.SemaphoreType.DMA((PEERS,)),
            pltpu.SemaphoreType.DMA((PEERS,)),
            pltpu.SemaphoreType.DMA((PEERS,)),
            pltpu.SemaphoreType.DMA,
            pltpu.SemaphoreType.DMA,
            pltpu.SemaphoreType.DMA,
            pltpu.SemaphoreType.DMA((LOCAL,)),
            pltpu.SemaphoreType.DMA((LOCAL,)),
            pltpu.SemaphoreType.DMA((LOCAL,)),
            pltpu.SemaphoreType.DMA,
        ],
        compiler_params=pltpu.CompilerParams(
            collective_id=0, has_side_effects=True, vmem_limit_bytes=60 * 1024 * 1024
        ),
    )(
        expert_ids.reshape(1, ROWS),
        samples,
        cotangent,
        weights,
    )
    return pl.pallas_call(
        hand_over,
        out_shape=outs,
        in_specs=[hbm] * 2,
        out_specs=(hbm, hbm),
        scratch_shapes=[
            pltpu.VMEM((ROWS, FEAT), bf16),
            pltpu.VMEM((LOCAL, 2, HALF, FEAT), bf16),
            pltpu.SemaphoreType.DMA((2 * LOCAL + GRAD_PARTS,)),
            pltpu.SemaphoreType.DMA((2 * LOCAL + GRAD_PARTS,)),
        ],
        compiler_params=pltpu.CompilerParams(vmem_limit_bytes=60 * 1024 * 1024),
    )(*results)


def solution(mesh):
    return jax.shard_map(
        on_device,
        mesh=mesh,
        in_specs=(
            P(("expert", "node"), None),
            P(("expert", "node"), None),
            P("expert", None, "node", None),
            P(("expert", "node"), None),
        ),
        out_specs=(P(("expert", "node"), None), P("expert", None, "node", None)),
        check_vma=False,
    )
```

```python
import functools
import math

import jax
import jax.numpy as jnp
from jax import lax
from jax.experimental import pallas as pl
from jax.experimental.pallas import tpu as pltpu
from jax.sharding import PartitionSpec as P

MESH = pl.DeviceIdType.MESH
ROWS = 768
FEAT = 512
HALF = 256
EXPERTS = 256
LOCAL = 4
CAP = 6
PAIR = LOCAL * CAP
MSG = 2 * PAIR
PEERS = 64
GROUP = 16
GROUPS = PEERS // GROUP
BLOCK = 4
PASS = 16
GROUP_ROWS = GROUP * CAP
GRAD_PARTS = 4
EXPERT_ROWS = PEERS * CAP


def sort_matrix():
    size = BLOCK * MSG
    row = lax.broadcasted_iota(jnp.int32, (1, size), 1)
    msg = sum((row >= (k + 1) * MSG).astype(jnp.int32) for k in range(BLOCK - 1))
    rest = row - msg * MSG
    kind = (rest >= PAIR).astype(jnp.int32)
    rest = rest - kind * PAIR
    local = sum((rest >= (k + 1) * CAP).astype(jnp.int32) for k in range(LOCAL - 1))
    slot = rest - local * CAP
    place = kind * (BLOCK * PAIR) + local * (BLOCK * CAP) + msg * CAP + slot
    return (lax.broadcasted_iota(jnp.int32, (size, size), 0) == place).astype(jnp.bfloat16)


def unsort_matrix():
    size = BLOCK * PAIR
    row = lax.broadcasted_iota(jnp.int32, (1, size), 1)
    local = sum((row >= (k + 1) * BLOCK * CAP).astype(jnp.int32) for k in range(LOCAL - 1))
    rest = row - local * (BLOCK * CAP)
    msg = sum((rest >= (k + 1) * CAP).astype(jnp.int32) for k in range(BLOCK - 1))
    slot = rest - msg * CAP
    place = msg * PAIR + local * CAP + slot
    return (lax.broadcasted_iota(jnp.int32, (size, size), 0) == place).astype(jnp.bfloat16)


def dot(a, b):
    return jnp.dot(a, b, preferred_element_type=jnp.float32)


def dot_t(a, b):
    return lax.dot_general(a, b, (((1,), (1,)), ((), ())), preferred_element_type=jnp.float32)


def t_dot(a, b):
    return lax.dot_general(a, b, (((0,), (0,)), ((), ())), preferred_element_type=jnp.float32)


def kernel(
    norm_scale,
    ids_hbm,
    samples_hbm,
    cot_hbm,
    weights_ref,
    grads_ref,
    wgrads_ref,
    ids_ref,
    samples_ref,
    cot_ref,
    into_ref,
    back_ref,
    send_buf,
    recv_buf,
    ysend_buf,
    yrecv_buf,
    g_group,
    slope0,
    act0,
    act1,
    pre0,
    pre1,
    wfull,
    wg_acc,
    wg_own,
    wg_send,
    wg_recv,
    wg_out,
    g_out,
    target_col,
    acc,
    in_sem,
    send_sem,
    recv_sem,
    ysend_sem,
    yrecv_sem,
    wlocal_sem,
    wsend_sem,
    wrecv_sem,
    gsend_sem,
    grecv_sem,
    out_sem,
    gout_sem,
):
    me = lax.axis_index("expert")
    node = lax.axis_index("node")
    my_x = lax.rem(me, 4)
    my_y = lax.rem(lax.div(me, 4), 4)
    my_z = lax.div(me, 16)

    def shifted(pos, sign):
        dx = lax.rem(pos, 4)
        dy = lax.rem(lax.div(pos, 4), 4)
        dz = lax.rem(lax.div(pos, 16) + dx + dy, 4)
        px = lax.rem(my_x + sign * dx + 4, 4)
        py = lax.rem(my_y + sign * dy + 4, 4)
        pz = lax.rem(my_z + sign * dz + 4, 4)
        return pz * 16 + py * 4 + px

    loads = [
        pltpu.make_async_copy(src, dst, in_sem.at[k])
        for k, (src, dst) in enumerate(
            ((ids_hbm, ids_ref), (samples_hbm, samples_ref), (cot_hbm, cot_ref))
        )
    ]
    for load in loads:
        load.start()
    barrier = pltpu.get_barrier_semaphore()

    for step in range(1, PEERS):
        peer = 16 * ((my_z + step // 16) & 3) + 4 * ((my_y + step // 4 % 4) & 3)
        peer = peer + ((my_x + step % 4) & 3)
        pl.semaphore_signal(barrier, inc=1, device_id=(peer, node), device_id_type=MESH)
    pl.semaphore_signal(barrier, inc=1, device_id=(me, 1 - node), device_id_type=MESH)

    my_half = pl.ds(pl.multiple_of(node * HALF, HALF), HALF)
    w_local = pltpu.make_async_copy(weights_ref, wfull.at[:, :, my_half, :], wlocal_sem)
    w_local.start()
    w_remote = pltpu.make_async_remote_copy(
        src_ref=weights_ref,
        dst_ref=wfull.at[:, :, my_half, :],
        send_sem=wsend_sem,
        recv_sem=wrecv_sem,
        device_id=(me, 1 - node),
        device_id_type=MESH,
    )

    loads[0].wait()
    ids = ids_ref[...]
    onehot = lax.broadcasted_iota(jnp.int32, (EXPERTS, ROWS), 0) == ids
    before = lax.broadcasted_iota(jnp.int32, (ROWS, ROWS), 0) < lax.broadcasted_iota(
        jnp.int32, (ROWS, ROWS), 1
    )
    earlier = dot(onehot.astype(jnp.bfloat16), before.astype(jnp.bfloat16))
    slot = jnp.sum(jnp.where(onehot, earlier, 0.0), axis=0, keepdims=True).astype(jnp.int32)
    owner = ids >> 2
    dx = ((owner & 3) - my_x + 4) & 3
    dy = (((owner >> 2) & 3) - my_y + 4) & 3
    dz = ((owner >> 4) - my_z + 4) & 3
    pos_of = ((dz - dx - dy + 8) & 3) * 16 + dy * 4 + dx
    target = pos_of * PAIR + (ids & 3) * CAP + slot

    def message(pos):
        return pltpu.make_async_remote_copy(
            src_ref=send_buf.at[pos],
            dst_ref=recv_buf.at[pos],
            send_sem=send_sem.at[pos // GROUP],
            recv_sem=recv_sem.at[pos // GROUP],
            device_id=(shifted(pos, 1), node),
            device_id_type=MESH,
        )

    def reply(pos):
        return pltpu.make_async_remote_copy(
            src_ref=ysend_buf.at[pos],
            dst_ref=yrecv_buf.at[pos],
            send_sem=ysend_sem.at[pos // GROUP],
            recv_sem=yrecv_sem.at[pos // GROUP],
            device_id=(shifted(pos, -1), node),
            device_id_type=MESH,
        )

    def over(low, high, action):
        def step(pos, carry):
            action(pos)
            return carry

        lax.fori_loop(low, high, step, 0)

    def send_all(copy, first, stride):
        def send(j):
            pos = first + lax.rem(j * stride, GROUP)

            @pl.when(pos != 0)
            def _():
                copy(pos).start()

        over(0, GROUP, send)

    def whole(group, first, count):
        part = pl.ds(group * GROUP + first, count)
        return (
            pltpu.make_async_remote_copy(
                src_ref=send_buf.at[part],
                dst_ref=recv_buf.at[part],
                send_sem=send_sem.at[group],
                recv_sem=recv_sem.at[group],
                device_id=(me, 1 - node),
                device_id_type=MESH,
            ),
            pltpu.make_async_remote_copy(
                src_ref=ysend_buf.at[part],
                dst_ref=yrecv_buf.at[part],
                send_sem=ysend_sem.at[group],
                recv_sem=yrecv_sem.at[group],
                device_id=(me, 1 - node),
                device_id_type=MESH,
            ),
        )

    def for_group(group, action):
        @pl.when(group == 0)
        def _():
            action(*whole(group, 1, GROUP - 1))

        @pl.when(group != 0)
        def _():
            action(*whole(group, 0, GROUP))

    loads[1].wait()
    loads[2].wait()

    def build(group):
        rows = lax.broadcasted_iota(jnp.int32, (GROUP * PAIR, ROWS), 0) + group * (GROUP * PAIR)
        pick = (rows == target).astype(jnp.bfloat16)
        feats = dot(pick, samples_ref[...])
        cots = dot(pick, cot_ref[...])
        for j in range(GROUP):
            part = slice(j * PAIR, (j + 1) * PAIR)
            both = jnp.concatenate([feats[part], cots[part]], 0).astype(jnp.bfloat16)
            send_buf[group * GROUP + j] = both

    build(0)
    recv_buf[0] = send_buf[0]
    pl.semaphore_wait(barrier, PEERS)
    send_all(message, 0, 5)
    w_remote.start()

    def dispatch(group, carry):
        build(group)
        send_all(message, group * GROUP, 5)
        return carry

    lax.fori_loop(1, GROUPS, dispatch, 0)
    into_ref[...] = sort_matrix()
    back_ref[...] = unsort_matrix()
    target_col[...] = jnp.broadcast_to(target.astype(jnp.float32), (128, ROWS)).T
    w_local.wait()
    w_remote.wait()

    def slope(val, sig):
        return sig * (1.0 + val * (1.0 - sig))

    def compute(count, first):
        for_group(first // GROUP, lambda messages, replies: messages.wait_recv())
        size = BLOCK * CAP
        ordered = []
        for block in range(count // BLOCK):
            received = recv_buf[pl.ds(first + block * BLOCK, BLOCK)]
            ordered.append(dot(into_ref[...], received.reshape(BLOCK * MSG, FEAT)))

        def rows_of(place):
            return jnp.concatenate([part[place * size : (place + 1) * size] for part in ordered], 0)

        rows = pl.ds(pl.multiple_of(first * CAP, 16), count * CAP)
        kept = slice(0, count * CAP)
        experts = range(LOCAL)
        for e in experts:
            act0[e, rows] = rows_of(e).astype(jnp.bfloat16)
            g_group[e, kept] = rows_of(LOCAL + e)
        val0 = [dot(act0[e, rows], wfull[e, 0]) for e in experts]
        for e in experts:
            sig = jax.nn.sigmoid(val0[e])
            act1[e, rows] = (val0[e] * sig).astype(jnp.bfloat16)
            slope0[e, kept] = slope(val0[e], sig)
        val1 = [dot(act1[e, rows], wfull[e, 1]) for e in experts]
        for e in experts:
            sig = jax.nn.sigmoid(val1[e])
            pre1[e, rows] = (g_group[e, kept] * slope(val1[e], sig)).astype(jnp.bfloat16)
        back1 = [dot_t(pre1[e, rows], wfull[e, 1]) for e in experts]
        for e in experts:
            grad = back1[e].astype(jnp.bfloat16).astype(jnp.float32)
            pre0[e, rows] = (grad * slope0[e, kept]).astype(jnp.bfloat16)
        back0 = [dot_t(pre0[e, rows], wfull[e, 0]) for e in experts]
        for block in range(count // BLOCK):
            part = slice(block * size, (block + 1) * size)
            by_expert = jnp.concatenate([back0[e][part] for e in experts], 0).astype(jnp.bfloat16)
            by_message = dot(back_ref[...], by_expert)
            for j in range(BLOCK):
                part = slice(j * PAIR, (j + 1) * PAIR)
                both = jnp.concatenate([by_message[part, :HALF], by_message[part, HALF:]], 0)
                ysend_buf[first + block * BLOCK + j] = both.astype(jnp.bfloat16)

        send_all(reply, first, 13)

    other_half = pl.ds(pl.multiple_of((1 - node) * HALF, HALF), HALF)

    def wg_copy(local):
        return pltpu.make_async_remote_copy(
            src_ref=wg_send.at[local],
            dst_ref=wg_recv.at[local],
            send_sem=gsend_sem.at[local],
            recv_sem=grecv_sem.at[local],
            device_id=(me, 1 - node),
            device_id_type=MESH,
        )

    layers = ((act0, pre0), (act1, pre1))
    span = EXPERT_ROWS // 2

    def first_grads(local, carry):
        for layer, (act, pre) in enumerate(layers):
            wg_acc[local, layer] = t_dot(act[local, :span], pre[local, :span])
        return carry

    def last_grads(local, carry):
        for layer, (act, pre) in enumerate(layers):
            for half, result in ((other_half, wg_send), (my_half, wg_own)):
                total = wg_acc[local, layer, half] + t_dot(
                    act[local, span:, half], pre[local, span:]
                )
                result[local, layer] = (total * norm_scale).astype(jnp.bfloat16)
        wg_copy(local).start()
        return carry

    def wg_store(local):
        return pltpu.make_async_copy(wg_out.at[local], wgrads_ref.at[local], out_sem.at[local])

    def add_grads(local, carry):
        wg_copy(local).wait()
        total = wg_own[local].astype(jnp.float32) + wg_recv[local].astype(jnp.float32)
        wg_out[local] = total.astype(jnp.bfloat16)
        wg_store(local).start()
        return carry

    def pass_of(step):
        compute(PASS, step * PASS)

        @pl.when(step == PEERS // PASS // 2 - 1)
        def _():
            lax.fori_loop(0, LOCAL, first_grads, 0)

    over(0, PEERS // PASS, pass_of)
    lax.fori_loop(0, LOCAL, last_grads, 0)
    yrecv_buf[0] = ysend_buf[0]

    acc[...] = jnp.zeros_like(acc)

    def combine(group, carry):
        for_group(group, lambda messages, replies: replies.wait_recv())
        received = yrecv_buf[pl.ds(group * GROUP, GROUP)].astype(jnp.float32)
        left = received[:, :PAIR].reshape(GROUP * PAIR, HALF)
        right = received[:, PAIR:].reshape(GROUP * PAIR, HALF)
        ordered = jnp.concatenate([left, right], 1).astype(jnp.bfloat16)
        columns = lax.broadcasted_iota(jnp.int32, (ROWS, GROUP * PAIR), 1) + group * (GROUP * PAIR)
        pick = (target_col[:, :1].astype(jnp.int32) == columns).astype(jnp.bfloat16)
        acc[...] += dot(pick, ordered)
        return carry

    lax.fori_loop(0, GROUPS - 1, combine, 0)
    lax.fori_loop(0, LOCAL, add_grads, 0)
    combine(GROUPS - 1, 0)
    g_out[...] = acc[...].astype(jnp.bfloat16)
    g_store = pltpu.make_async_copy(g_out, grads_ref, gout_sem)
    g_store.start()

    def drain(group):
        for_group(group, lambda messages, replies: messages.wait_send())
        for_group(group, lambda messages, replies: replies.wait_send())

    over(0, GROUPS, drain)
    over(0, LOCAL, lambda local: wg_store(local).wait())
    g_store.wait()


def hand_over(grads_in, wgrads_in, grads_out, wgrads_out, grads_buf, wgrads_buf, in_sem, out_sem):
    size = ROWS // GRAD_PARTS
    rows = [pl.ds(k * size, size) for k in range(GRAD_PARTS)]
    parts = [
        (src.at[part], buf.at[part], dst.at[part])
        for src, buf, dst, all_parts in (
            (wgrads_in, wgrads_buf, wgrads_out, [(k, j) for k in range(LOCAL) for j in range(2)]),
            (grads_in, grads_buf, grads_out, rows),
        )
        for part in all_parts
    ]
    reads = [pltpu.make_async_copy(p[0], p[1], in_sem.at[k]) for k, p in enumerate(parts)]
    writes = [pltpu.make_async_copy(p[1], p[2], out_sem.at[k]) for k, p in enumerate(parts)]
    for copy in reads:
        copy.start()
    for read, write in zip(reads, writes):
        read.wait()
        write.start()
    for copy in writes:
        copy.wait()


def on_device(samples, cotangent, weights, expert_ids):
    bf16 = jnp.bfloat16
    node_count = lax.axis_size("node")
    norm_scale = 1.0 / math.sqrt(ROWS * node_count / LOCAL)
    hbm = pl.BlockSpec(memory_space=pltpu.HBM)
    outs = (
        jax.ShapeDtypeStruct((ROWS, FEAT), bf16),
        jax.ShapeDtypeStruct((LOCAL, 2, HALF, FEAT), bf16),
    )
    results = pl.pallas_call(
        functools.partial(kernel, norm_scale),
        out_shape=outs,
        in_specs=[hbm] * 4,
        out_specs=(hbm, hbm),
        scratch_shapes=[
            pltpu.VMEM((1, ROWS), jnp.int32),
            pltpu.VMEM((ROWS, FEAT), bf16),
            pltpu.VMEM((ROWS, FEAT), bf16),
            pltpu.VMEM((BLOCK * MSG, BLOCK * MSG), bf16),
            pltpu.VMEM((BLOCK * PAIR, BLOCK * PAIR), bf16),
            pltpu.VMEM((PEERS, MSG, FEAT), bf16),
            pltpu.VMEM((PEERS, MSG, FEAT), bf16),
            pltpu.VMEM((PEERS, MSG, HALF), bf16),
            pltpu.VMEM((PEERS, MSG, HALF), bf16),
            pltpu.VMEM((LOCAL, GROUP_ROWS, FEAT), jnp.float32),
            pltpu.VMEM((LOCAL, GROUP_ROWS, FEAT), jnp.float32),
            pltpu.VMEM((LOCAL, EXPERT_ROWS, FEAT), bf16),
            pltpu.VMEM((LOCAL, EXPERT_ROWS, FEAT), bf16),
            pltpu.VMEM((LOCAL, EXPERT_ROWS, FEAT), bf16),
            pltpu.VMEM((LOCAL, EXPERT_ROWS, FEAT), bf16),
            pltpu.VMEM((LOCAL, 2, FEAT, FEAT), bf16),
            pltpu.VMEM((LOCAL, 2, FEAT, FEAT), jnp.float32),
            pltpu.VMEM((LOCAL, 2, HALF, FEAT), bf16),
            pltpu.VMEM((LOCAL, 2, HALF, FEAT), bf16),
            pltpu.VMEM((LOCAL, 2, HALF, FEAT), bf16),
            pltpu.VMEM((LOCAL, 2, HALF, FEAT), bf16),
            pltpu.VMEM((ROWS, FEAT), bf16),
            pltpu.VMEM((ROWS, 128), jnp.float32),
            pltpu.VMEM((ROWS, FEAT), jnp.float32),
            pltpu.SemaphoreType.DMA((3,)),
            pltpu.SemaphoreType.DMA((GROUPS,)),
            pltpu.SemaphoreType.DMA((GROUPS,)),
            pltpu.SemaphoreType.DMA((GROUPS,)),
            pltpu.SemaphoreType.DMA((GROUPS,)),
            pltpu.SemaphoreType.DMA,
            pltpu.SemaphoreType.DMA,
            pltpu.SemaphoreType.DMA,
            pltpu.SemaphoreType.DMA((LOCAL,)),
            pltpu.SemaphoreType.DMA((LOCAL,)),
            pltpu.SemaphoreType.DMA((LOCAL,)),
            pltpu.SemaphoreType.DMA,
        ],
        compiler_params=pltpu.CompilerParams(
            collective_id=0, has_side_effects=True, vmem_limit_bytes=60 * 1024 * 1024
        ),
    )(
        expert_ids.reshape(1, ROWS),
        samples,
        cotangent,
        weights,
    )
    return pl.pallas_call(
        hand_over,
        out_shape=outs,
        in_specs=[hbm] * 2,
        out_specs=(hbm, hbm),
        scratch_shapes=[
            pltpu.VMEM((ROWS, FEAT), bf16),
            pltpu.VMEM((LOCAL, 2, HALF, FEAT), bf16),
            pltpu.SemaphoreType.DMA((2 * LOCAL + GRAD_PARTS,)),
            pltpu.SemaphoreType.DMA((2 * LOCAL + GRAD_PARTS,)),
        ],
        compiler_params=pltpu.CompilerParams(vmem_limit_bytes=60 * 1024 * 1024),
    )(*results)


def solution(mesh):
    return jax.shard_map(
        on_device,
        mesh=mesh,
        in_specs=(
            P(("expert", "node"), None),
            P(("expert", "node"), None),
            P("expert", None, "node", None),
            P(("expert", "node"), None),
        ),
        out_specs=(P(("expert", "node"), None), P("expert", None, "node", None)),
        check_vma=False,
    )
```

```python
import functools
import math

import jax
import jax.numpy as jnp
from jax import lax
from jax.experimental import pallas as pl
from jax.experimental.pallas import tpu as pltpu
from jax.sharding import PartitionSpec as P

MESH = pl.DeviceIdType.MESH
ROWS = 768
FEAT = 512
HALF = 256
EXPERTS = 256
LOCAL = 4
CAP = 6
PAIR = LOCAL * CAP
MSG = 2 * PAIR
PEERS = 64
GROUP = 16
GROUPS = PEERS // GROUP
BLOCK = 4
PASS = 16
GROUP_ROWS = GROUP * CAP
GRAD_PARTS = 4
EXPERT_ROWS = PEERS * CAP


def sort_matrix():
    size = BLOCK * MSG
    row = lax.broadcasted_iota(jnp.int32, (1, size), 1)
    msg = sum((row >= (k + 1) * MSG).astype(jnp.int32) for k in range(BLOCK - 1))
    rest = row - msg * MSG
    kind = (rest >= PAIR).astype(jnp.int32)
    rest = rest - kind * PAIR
    local = sum((rest >= (k + 1) * CAP).astype(jnp.int32) for k in range(LOCAL - 1))
    slot = rest - local * CAP
    place = kind * (BLOCK * PAIR) + local * (BLOCK * CAP) + msg * CAP + slot
    return (lax.broadcasted_iota(jnp.int32, (size, size), 0) == place).astype(jnp.bfloat16)


def unsort_matrix():
    size = BLOCK * PAIR
    row = lax.broadcasted_iota(jnp.int32, (1, size), 1)
    local = sum((row >= (k + 1) * BLOCK * CAP).astype(jnp.int32) for k in range(LOCAL - 1))
    rest = row - local * (BLOCK * CAP)
    msg = sum((rest >= (k + 1) * CAP).astype(jnp.int32) for k in range(BLOCK - 1))
    slot = rest - msg * CAP
    place = msg * PAIR + local * CAP + slot
    return (lax.broadcasted_iota(jnp.int32, (size, size), 0) == place).astype(jnp.bfloat16)


def dot(a, b):
    return jnp.dot(a, b, preferred_element_type=jnp.float32)


def dot_t(a, b):
    return lax.dot_general(a, b, (((1,), (1,)), ((), ())), preferred_element_type=jnp.float32)


def t_dot(a, b):
    return lax.dot_general(a, b, (((0,), (0,)), ((), ())), preferred_element_type=jnp.float32)


def kernel(
    norm_scale,
    ids_hbm,
    samples_hbm,
    cot_hbm,
    weights_ref,
    grads_ref,
    wgrads_ref,
    ids_ref,
    samples_ref,
    cot_ref,
    into_ref,
    back_ref,
    send_buf,
    recv_buf,
    ysend_buf,
    yrecv_buf,
    g_group,
    slope0,
    act0,
    act1,
    pre0,
    pre1,
    wfull,
    wg_acc,
    wg_own,
    wg_send,
    wg_recv,
    wg_out,
    g_out,
    target_col,
    acc,
    in_sem,
    send_sem,
    recv_sem,
    ysend_sem,
    yrecv_sem,
    wlocal_sem,
    wsend_sem,
    wrecv_sem,
    gsend_sem,
    grecv_sem,
    out_sem,
    gout_sem,
):
    me = lax.axis_index("expert")
    node = lax.axis_index("node")
    my_x = lax.rem(me, 4)
    my_y = lax.rem(lax.div(me, 4), 4)
    my_z = lax.div(me, 16)

    def shifted(pos, sign):
        dx = lax.rem(pos, 4)
        dy = lax.rem(lax.div(pos, 4), 4)
        dz = lax.rem(lax.div(pos, 16) + dx + dy, 4)
        px = lax.rem(my_x + sign * dx + 4, 4)
        py = lax.rem(my_y + sign * dy + 4, 4)
        pz = lax.rem(my_z + sign * dz + 4, 4)
        return pz * 16 + py * 4 + px

    loads = [
        pltpu.make_async_copy(src, dst, in_sem.at[k])
        for k, (src, dst) in enumerate(
            ((ids_hbm, ids_ref), (samples_hbm, samples_ref), (cot_hbm, cot_ref))
        )
    ]
    for load in loads:
        load.start()
    barrier = pltpu.get_barrier_semaphore()

    for step in range(1, PEERS):
        peer = 16 * ((my_z + step // 16) & 3) + 4 * ((my_y + step // 4 % 4) & 3)
        peer = peer + ((my_x + step % 4) & 3)
        pl.semaphore_signal(barrier, inc=1, device_id=(peer, node), device_id_type=MESH)
    pl.semaphore_signal(barrier, inc=1, device_id=(me, 1 - node), device_id_type=MESH)

    my_half = pl.ds(pl.multiple_of(node * HALF, HALF), HALF)
    w_local = pltpu.make_async_copy(weights_ref, wfull.at[:, :, my_half, :], wlocal_sem)
    w_local.start()
    w_remote = pltpu.make_async_remote_copy(
        src_ref=weights_ref,
        dst_ref=wfull.at[:, :, my_half, :],
        send_sem=wsend_sem,
        recv_sem=wrecv_sem,
        device_id=(me, 1 - node),
        device_id_type=MESH,
    )

    loads[0].wait()
    ids = ids_ref[...]
    onehot = lax.broadcasted_iota(jnp.int32, (EXPERTS, ROWS), 0) == ids
    before = lax.broadcasted_iota(jnp.int32, (ROWS, ROWS), 0) < lax.broadcasted_iota(
        jnp.int32, (ROWS, ROWS), 1
    )
    earlier = dot(onehot.astype(jnp.bfloat16), before.astype(jnp.bfloat16))
    slot = jnp.sum(jnp.where(onehot, earlier, 0.0), axis=0, keepdims=True).astype(jnp.int32)
    owner = ids >> 2
    dx = ((owner & 3) - my_x + 4) & 3
    dy = (((owner >> 2) & 3) - my_y + 4) & 3
    dz = ((owner >> 4) - my_z + 4) & 3
    pos_of = ((dz - dx - dy + 8) & 3) * 16 + dy * 4 + dx
    target = pos_of * PAIR + (ids & 3) * CAP + slot

    def message(pos):
        return pltpu.make_async_remote_copy(
            src_ref=send_buf.at[pos],
            dst_ref=recv_buf.at[pos],
            send_sem=send_sem.at[pos // GROUP],
            recv_sem=recv_sem.at[pos // GROUP],
            device_id=(shifted(pos, 1), node),
            device_id_type=MESH,
        )

    def reply(pos):
        return pltpu.make_async_remote_copy(
            src_ref=ysend_buf.at[pos],
            dst_ref=yrecv_buf.at[pos],
            send_sem=ysend_sem.at[pos // GROUP],
            recv_sem=yrecv_sem.at[pos // GROUP],
            device_id=(shifted(pos, -1), node),
            device_id_type=MESH,
        )

    def over(low, high, action):
        def step(pos, carry):
            action(pos)
            return carry

        lax.fori_loop(low, high, step, 0)

    def send_all(copy, first, stride):
        def send(j):
            pos = first + lax.rem(j * stride, GROUP)

            @pl.when(pos != 0)
            def _():
                copy(pos).start()

        over(0, GROUP, send)

    def whole(group, first, count):
        part = pl.ds(group * GROUP + first, count)
        return (
            pltpu.make_async_remote_copy(
                src_ref=send_buf.at[part],
                dst_ref=recv_buf.at[part],
                send_sem=send_sem.at[group],
                recv_sem=recv_sem.at[group],
                device_id=(me, 1 - node),
                device_id_type=MESH,
            ),
            pltpu.make_async_remote_copy(
                src_ref=ysend_buf.at[part],
                dst_ref=yrecv_buf.at[part],
                send_sem=ysend_sem.at[group],
                recv_sem=yrecv_sem.at[group],
                device_id=(me, 1 - node),
                device_id_type=MESH,
            ),
        )

    def for_group(group, action):
        @pl.when(group == 0)
        def _():
            action(*whole(group, 1, GROUP - 1))

        @pl.when(group != 0)
        def _():
            action(*whole(group, 0, GROUP))

    loads[1].wait()
    loads[2].wait()

    def build(group):
        rows = lax.broadcasted_iota(jnp.int32, (GROUP * PAIR, ROWS), 0) + group * (GROUP * PAIR)
        pick = (rows == target).astype(jnp.bfloat16)
        feats = dot(pick, samples_ref[...])
        cots = dot(pick, cot_ref[...])
        for j in range(GROUP):
            part = slice(j * PAIR, (j + 1) * PAIR)
            both = jnp.concatenate([feats[part], cots[part]], 0).astype(jnp.bfloat16)
            send_buf[group * GROUP + j] = both

    build(0)
    recv_buf[0] = send_buf[0]
    pl.semaphore_wait(barrier, PEERS)
    send_all(message, 0, 5)
    w_remote.start()

    def dispatch(group, carry):
        build(group)
        send_all(message, group * GROUP, 5)
        return carry

    lax.fori_loop(1, GROUPS, dispatch, 0)
    into_ref[...] = sort_matrix()
    back_ref[...] = unsort_matrix()
    target_col[...] = jnp.broadcast_to(target.astype(jnp.float32), (128, ROWS)).T
    w_local.wait()
    w_remote.wait()

    def slope(val, sig):
        return sig * (1.0 + val * (1.0 - sig))

    def compute(count, first):
        for_group(first // GROUP, lambda messages, replies: messages.wait_recv())
        size = BLOCK * CAP
        ordered = []
        for block in range(count // BLOCK):
            received = recv_buf[pl.ds(first + block * BLOCK, BLOCK)]
            ordered.append(dot(into_ref[...], received.reshape(BLOCK * MSG, FEAT)))

        def rows_of(place):
            return jnp.concatenate([part[place * size : (place + 1) * size] for part in ordered], 0)

        rows = pl.ds(pl.multiple_of(first * CAP, 16), count * CAP)
        kept = slice(0, count * CAP)
        experts = range(LOCAL)
        for e in experts:
            act0[e, rows] = rows_of(e).astype(jnp.bfloat16)
            g_group[e, kept] = rows_of(LOCAL + e)
        val0 = [dot(act0[e, rows], wfull[e, 0]) for e in experts]
        for e in experts:
            sig = jax.nn.sigmoid(val0[e])
            act1[e, rows] = (val0[e] * sig).astype(jnp.bfloat16)
            slope0[e, kept] = slope(val0[e], sig)
        val1 = [dot(act1[e, rows], wfull[e, 1]) for e in experts]
        for e in experts:
            sig = jax.nn.sigmoid(val1[e])
            pre1[e, rows] = (g_group[e, kept] * slope(val1[e], sig)).astype(jnp.bfloat16)
        back1 = [dot_t(pre1[e, rows], wfull[e, 1]) for e in experts]
        for e in experts:
            grad = back1[e].astype(jnp.bfloat16).astype(jnp.float32)
            pre0[e, rows] = (grad * slope0[e, kept]).astype(jnp.bfloat16)
        back0 = [dot_t(pre0[e, rows], wfull[e, 0]) for e in experts]
        for block in range(count // BLOCK):
            part = slice(block * size, (block + 1) * size)
            by_expert = jnp.concatenate([back0[e][part] for e in experts], 0).astype(jnp.bfloat16)
            by_message = dot(back_ref[...], by_expert)
            for j in range(BLOCK):
                part = slice(j * PAIR, (j + 1) * PAIR)
                both = jnp.concatenate([by_message[part, :HALF], by_message[part, HALF:]], 0)
                ysend_buf[first + block * BLOCK + j] = both.astype(jnp.bfloat16)

        send_all(reply, first, 9)

    other_half = pl.ds(pl.multiple_of((1 - node) * HALF, HALF), HALF)

    def wg_copy(local):
        return pltpu.make_async_remote_copy(
            src_ref=wg_send.at[local],
            dst_ref=wg_recv.at[local],
            send_sem=gsend_sem.at[local],
            recv_sem=grecv_sem.at[local],
            device_id=(me, 1 - node),
            device_id_type=MESH,
        )

    layers = ((act0, pre0), (act1, pre1))
    span = EXPERT_ROWS // 2

    def first_grads(local, carry):
        for layer, (act, pre) in enumerate(layers):
            wg_acc[local, layer] = t_dot(act[local, :span], pre[local, :span])
        return carry

    def last_grads(local, carry):
        for layer, (act, pre) in enumerate(layers):
            for half, result in ((other_half, wg_send), (my_half, wg_own)):
                total = wg_acc[local, layer, half] + t_dot(
                    act[local, span:, half], pre[local, span:]
                )
                result[local, layer] = (total * norm_scale).astype(jnp.bfloat16)
        wg_copy(local).start()
        return carry

    def wg_store(local):
        return pltpu.make_async_copy(wg_out.at[local], wgrads_ref.at[local], out_sem.at[local])

    def add_grads(local, carry):
        wg_copy(local).wait()
        total = wg_own[local].astype(jnp.float32) + wg_recv[local].astype(jnp.float32)
        wg_out[local] = total.astype(jnp.bfloat16)
        wg_store(local).start()
        return carry

    def pass_of(step):
        compute(PASS, step * PASS)

        @pl.when(step == PEERS // PASS // 2 - 1)
        def _():
            lax.fori_loop(0, LOCAL, first_grads, 0)

    over(0, PEERS // PASS, pass_of)
    lax.fori_loop(0, LOCAL, last_grads, 0)
    yrecv_buf[0] = ysend_buf[0]

    acc[...] = jnp.zeros_like(acc)

    def combined(group):
        for_group(group, lambda messages, replies: replies.wait_recv())
        received = yrecv_buf[pl.ds(group * GROUP, GROUP)].astype(jnp.float32)
        left = received[:, :PAIR].reshape(GROUP * PAIR, HALF)
        right = received[:, PAIR:].reshape(GROUP * PAIR, HALF)
        ordered = jnp.concatenate([left, right], 1).astype(jnp.bfloat16)
        columns = lax.broadcasted_iota(jnp.int32, (ROWS, GROUP * PAIR), 1) + group * (GROUP * PAIR)
        pick = (target_col[:, :1].astype(jnp.int32) == columns).astype(jnp.bfloat16)
        return dot(pick, ordered)

    def combine(group, carry):
        acc[...] += combined(group)
        return carry

    lax.fori_loop(0, GROUPS - 1, combine, 0)
    lax.fori_loop(0, LOCAL, add_grads, 0)
    g_out[...] = (acc[...] + combined(GROUPS - 1)).astype(jnp.bfloat16)
    g_store = pltpu.make_async_copy(g_out, grads_ref, gout_sem)
    g_store.start()

    def drain(group):
        for_group(group, lambda messages, replies: messages.wait_send())
        for_group(group, lambda messages, replies: replies.wait_send())

    over(0, GROUPS, drain)
    over(0, LOCAL, lambda local: wg_store(local).wait())
    g_store.wait()


def hand_over(grads_in, wgrads_in, grads_out, wgrads_out, grads_buf, wgrads_buf, in_sem, out_sem):
    size = ROWS // GRAD_PARTS
    rows = [pl.ds(k * size, size) for k in range(GRAD_PARTS)]
    parts = [
        (src.at[part], buf.at[part], dst.at[part])
        for src, buf, dst, all_parts in (
            (wgrads_in, wgrads_buf, wgrads_out, [(k, j) for k in range(LOCAL) for j in range(2)]),
            (grads_in, grads_buf, grads_out, rows),
        )
        for part in all_parts
    ]
    reads = [pltpu.make_async_copy(p[0], p[1], in_sem.at[k]) for k, p in enumerate(parts)]
    writes = [pltpu.make_async_copy(p[1], p[2], out_sem.at[k]) for k, p in enumerate(parts)]
    for copy in reads:
        copy.start()
    for read, write in zip(reads, writes):
        read.wait()
        write.start()
    for copy in writes:
        copy.wait()


def on_device(samples, cotangent, weights, expert_ids):
    bf16 = jnp.bfloat16
    node_count = lax.axis_size("node")
    norm_scale = 1.0 / math.sqrt(ROWS * node_count / LOCAL)
    hbm = pl.BlockSpec(memory_space=pltpu.HBM)
    outs = (
        jax.ShapeDtypeStruct((ROWS, FEAT), bf16),
        jax.ShapeDtypeStruct((LOCAL, 2, HALF, FEAT), bf16),
    )
    results = pl.pallas_call(
        functools.partial(kernel, norm_scale),
        out_shape=outs,
        in_specs=[hbm] * 4,
        out_specs=(hbm, hbm),
        scratch_shapes=[
            pltpu.VMEM((1, ROWS), jnp.int32),
            pltpu.VMEM((ROWS, FEAT), bf16),
            pltpu.VMEM((ROWS, FEAT), bf16),
            pltpu.VMEM((BLOCK * MSG, BLOCK * MSG), bf16),
            pltpu.VMEM((BLOCK * PAIR, BLOCK * PAIR), bf16),
            pltpu.VMEM((PEERS, MSG, FEAT), bf16),
            pltpu.VMEM((PEERS, MSG, FEAT), bf16),
            pltpu.VMEM((PEERS, MSG, HALF), bf16),
            pltpu.VMEM((PEERS, MSG, HALF), bf16),
            pltpu.VMEM((LOCAL, GROUP_ROWS, FEAT), jnp.float32),
            pltpu.VMEM((LOCAL, GROUP_ROWS, FEAT), jnp.float32),
            pltpu.VMEM((LOCAL, EXPERT_ROWS, FEAT), bf16),
            pltpu.VMEM((LOCAL, EXPERT_ROWS, FEAT), bf16),
            pltpu.VMEM((LOCAL, EXPERT_ROWS, FEAT), bf16),
            pltpu.VMEM((LOCAL, EXPERT_ROWS, FEAT), bf16),
            pltpu.VMEM((LOCAL, 2, FEAT, FEAT), bf16),
            pltpu.VMEM((LOCAL, 2, FEAT, FEAT), jnp.float32),
            pltpu.VMEM((LOCAL, 2, HALF, FEAT), bf16),
            pltpu.VMEM((LOCAL, 2, HALF, FEAT), bf16),
            pltpu.VMEM((LOCAL, 2, HALF, FEAT), bf16),
            pltpu.VMEM((LOCAL, 2, HALF, FEAT), bf16),
            pltpu.VMEM((ROWS, FEAT), bf16),
            pltpu.VMEM((ROWS, 128), jnp.float32),
            pltpu.VMEM((ROWS, FEAT), jnp.float32),
            pltpu.SemaphoreType.DMA((3,)),
            pltpu.SemaphoreType.DMA((GROUPS,)),
            pltpu.SemaphoreType.DMA((GROUPS,)),
            pltpu.SemaphoreType.DMA((GROUPS,)),
            pltpu.SemaphoreType.DMA((GROUPS,)),
            pltpu.SemaphoreType.DMA,
            pltpu.SemaphoreType.DMA,
            pltpu.SemaphoreType.DMA,
            pltpu.SemaphoreType.DMA((LOCAL,)),
            pltpu.SemaphoreType.DMA((LOCAL,)),
            pltpu.SemaphoreType.DMA((LOCAL,)),
            pltpu.SemaphoreType.DMA,
        ],
        compiler_params=pltpu.CompilerParams(
            collective_id=0, has_side_effects=True, vmem_limit_bytes=60 * 1024 * 1024
        ),
    )(
        expert_ids.reshape(1, ROWS),
        samples,
        cotangent,
        weights,
    )
    return pl.pallas_call(
        hand_over,
        out_shape=outs,
        in_specs=[hbm] * 2,
        out_specs=(hbm, hbm),
        scratch_shapes=[
            pltpu.VMEM((ROWS, FEAT), bf16),
            pltpu.VMEM((LOCAL, 2, HALF, FEAT), bf16),
            pltpu.SemaphoreType.DMA((2 * LOCAL + GRAD_PARTS,)),
            pltpu.SemaphoreType.DMA((2 * LOCAL + GRAD_PARTS,)),
        ],
        compiler_params=pltpu.CompilerParams(vmem_limit_bytes=60 * 1024 * 1024),
    )(*results)


def solution(mesh):
    return jax.shard_map(
        on_device,
        mesh=mesh,
        in_specs=(
            P(("expert", "node"), None),
            P(("expert", "node"), None),
            P("expert", None, "node", None),
            P(("expert", "node"), None),
        ),
        out_specs=(P(("expert", "node"), None), P("expert", None, "node", None)),
        check_vma=False,
    )
```

```python
import functools
import math

import jax
import jax.numpy as jnp
from jax import lax
from jax.experimental import pallas as pl
from jax.experimental.pallas import tpu as pltpu
from jax.sharding import PartitionSpec as P

MESH = pl.DeviceIdType.MESH
ROWS = 768
FEAT = 512
HALF = 256
EXPERTS = 256
LOCAL = 4
CAP = 6
PAIR = LOCAL * CAP
MSG = 2 * PAIR
PEERS = 64
GROUP = 16
GROUPS = PEERS // GROUP
BLOCK = 4
PASS = 16
GROUP_ROWS = GROUP * CAP
GRAD_PARTS = 4
EXPERT_ROWS = PEERS * CAP


def sort_matrix():
    size = BLOCK * MSG
    row = lax.broadcasted_iota(jnp.int32, (1, size), 1)
    msg = sum((row >= (k + 1) * MSG).astype(jnp.int32) for k in range(BLOCK - 1))
    rest = row - msg * MSG
    kind = (rest >= PAIR).astype(jnp.int32)
    rest = rest - kind * PAIR
    local = sum((rest >= (k + 1) * CAP).astype(jnp.int32) for k in range(LOCAL - 1))
    slot = rest - local * CAP
    place = kind * (BLOCK * PAIR) + local * (BLOCK * CAP) + msg * CAP + slot
    return (lax.broadcasted_iota(jnp.int32, (size, size), 0) == place).astype(jnp.bfloat16)


def unsort_matrix():
    size = BLOCK * PAIR
    row = lax.broadcasted_iota(jnp.int32, (1, size), 1)
    local = sum((row >= (k + 1) * BLOCK * CAP).astype(jnp.int32) for k in range(LOCAL - 1))
    rest = row - local * (BLOCK * CAP)
    msg = sum((rest >= (k + 1) * CAP).astype(jnp.int32) for k in range(BLOCK - 1))
    slot = rest - msg * CAP
    place = msg * PAIR + local * CAP + slot
    return (lax.broadcasted_iota(jnp.int32, (size, size), 0) == place).astype(jnp.bfloat16)


def dot(a, b):
    return jnp.dot(a, b, preferred_element_type=jnp.float32)


def dot_t(a, b):
    return lax.dot_general(a, b, (((1,), (1,)), ((), ())), preferred_element_type=jnp.float32)


def t_dot(a, b):
    return lax.dot_general(a, b, (((0,), (0,)), ((), ())), preferred_element_type=jnp.float32)


def kernel(
    norm_scale,
    ids_hbm,
    samples_hbm,
    cot_hbm,
    weights_ref,
    grads_ref,
    wgrads_ref,
    ids_ref,
    samples_ref,
    cot_ref,
    into_ref,
    back_ref,
    send_buf,
    recv_buf,
    ysend_buf,
    yrecv_buf,
    g_group,
    slope0,
    act0,
    act1,
    pre0,
    pre1,
    wfull,
    wg_acc,
    wg_own,
    wg_send,
    wg_recv,
    wg_out,
    g_out,
    target_col,
    acc,
    in_sem,
    send_sem,
    recv_sem,
    ysend_sem,
    yrecv_sem,
    wlocal_sem,
    wsend_sem,
    wrecv_sem,
    gsend_sem,
    grecv_sem,
    out_sem,
    gout_sem,
):
    me = lax.axis_index("expert")
    node = lax.axis_index("node")
    my_x = lax.rem(me, 4)
    my_y = lax.rem(lax.div(me, 4), 4)
    my_z = lax.div(me, 16)

    def shifted(pos, sign):
        dx = lax.rem(pos, 4)
        dy = lax.rem(lax.div(pos, 4), 4)
        dz = lax.rem(lax.div(pos, 16) + dx + dy, 4)
        px = lax.rem(my_x + sign * dx + 4, 4)
        py = lax.rem(my_y + sign * dy + 4, 4)
        pz = lax.rem(my_z + sign * dz + 4, 4)
        return pz * 16 + py * 4 + px

    loads = [
        pltpu.make_async_copy(src, dst, in_sem.at[k])
        for k, (src, dst) in enumerate(
            ((ids_hbm, ids_ref), (samples_hbm, samples_ref), (cot_hbm, cot_ref))
        )
    ]
    for load in loads:
        load.start()
    barrier = pltpu.get_barrier_semaphore()

    for step in range(1, PEERS):
        peer = 16 * ((my_z + step // 16) & 3) + 4 * ((my_y + step // 4 % 4) & 3)
        peer = peer + ((my_x + step % 4) & 3)
        pl.semaphore_signal(barrier, inc=1, device_id=(peer, node), device_id_type=MESH)
    pl.semaphore_signal(barrier, inc=1, device_id=(me, 1 - node), device_id_type=MESH)

    my_half = pl.ds(pl.multiple_of(node * HALF, HALF), HALF)
    w_local = pltpu.make_async_copy(weights_ref, wfull.at[:, :, my_half, :], wlocal_sem)
    w_local.start()
    w_remote = pltpu.make_async_remote_copy(
        src_ref=weights_ref,
        dst_ref=wfull.at[:, :, my_half, :],
        send_sem=wsend_sem,
        recv_sem=wrecv_sem,
        device_id=(me, 1 - node),
        device_id_type=MESH,
    )

    loads[0].wait()
    ids = ids_ref[...]
    onehot = lax.broadcasted_iota(jnp.int32, (EXPERTS, ROWS), 0) == ids
    before = lax.broadcasted_iota(jnp.int32, (ROWS, ROWS), 0) < lax.broadcasted_iota(
        jnp.int32, (ROWS, ROWS), 1
    )
    earlier = dot(onehot.astype(jnp.bfloat16), before.astype(jnp.bfloat16))
    slot = jnp.sum(jnp.where(onehot, earlier, 0.0), axis=0, keepdims=True).astype(jnp.int32)
    owner = ids >> 2
    dx = ((owner & 3) - my_x + 4) & 3
    dy = (((owner >> 2) & 3) - my_y + 4) & 3
    dz = ((owner >> 4) - my_z + 4) & 3
    pos_of = ((dz - dx - dy + 8) & 3) * 16 + dy * 4 + dx
    target = pos_of * PAIR + (ids & 3) * CAP + slot

    def message(pos):
        return pltpu.make_async_remote_copy(
            src_ref=send_buf.at[pos],
            dst_ref=recv_buf.at[pos],
            send_sem=send_sem.at[pos // GROUP],
            recv_sem=recv_sem.at[pos // GROUP],
            device_id=(shifted(pos, 1), node),
            device_id_type=MESH,
        )

    def reply(pos):
        return pltpu.make_async_remote_copy(
            src_ref=ysend_buf.at[pos],
            dst_ref=yrecv_buf.at[pos],
            send_sem=ysend_sem.at[pos // GROUP],
            recv_sem=yrecv_sem.at[pos // GROUP],
            device_id=(shifted(pos, -1), node),
            device_id_type=MESH,
        )

    def over(low, high, action):
        def step(pos, carry):
            action(pos)
            return carry

        lax.fori_loop(low, high, step, 0)

    def send_all(copy, first, stride):
        @pl.when(first != 0)
        def _():
            copy(first).start()

        for j in range(1, GROUP):
            copy(first + j * stride % GROUP).start()

    def whole(group, first, count):
        part = pl.ds(group * GROUP + first, count)
        return (
            pltpu.make_async_remote_copy(
                src_ref=send_buf.at[part],
                dst_ref=recv_buf.at[part],
                send_sem=send_sem.at[group],
                recv_sem=recv_sem.at[group],
                device_id=(me, 1 - node),
                device_id_type=MESH,
            ),
            pltpu.make_async_remote_copy(
                src_ref=ysend_buf.at[part],
                dst_ref=yrecv_buf.at[part],
                send_sem=ysend_sem.at[group],
                recv_sem=yrecv_sem.at[group],
                device_id=(me, 1 - node),
                device_id_type=MESH,
            ),
        )

    def for_group(group, action):
        @pl.when(group == 0)
        def _():
            action(*whole(group, 1, GROUP - 1))

        @pl.when(group != 0)
        def _():
            action(*whole(group, 0, GROUP))

    loads[1].wait()
    loads[2].wait()

    def build(group):
        rows = lax.broadcasted_iota(jnp.int32, (GROUP * PAIR, ROWS), 0) + group * (GROUP * PAIR)
        pick = (rows == target).astype(jnp.bfloat16)
        feats = dot(pick, samples_ref[...])
        cots = dot(pick, cot_ref[...])
        for j in range(GROUP):
            part = slice(j * PAIR, (j + 1) * PAIR)
            both = jnp.concatenate([feats[part], cots[part]], 0).astype(jnp.bfloat16)
            send_buf[group * GROUP + j] = both

    build(0)
    recv_buf[0] = send_buf[0]
    pl.semaphore_wait(barrier, PEERS)
    send_all(message, 0, 5)
    w_remote.start()

    def dispatch(group, carry):
        build(group)
        send_all(message, group * GROUP, 5)
        return carry

    lax.fori_loop(1, GROUPS, dispatch, 0)
    into_ref[...] = sort_matrix()
    back_ref[...] = unsort_matrix()
    target_col[...] = jnp.broadcast_to(target.astype(jnp.float32), (128, ROWS)).T
    w_local.wait()
    w_remote.wait()

    def slope(val, sig):
        return sig * (1.0 + val * (1.0 - sig))

    def compute(count, first):
        for_group(first // GROUP, lambda messages, replies: messages.wait_recv())
        size = BLOCK * CAP
        ordered = []
        for block in range(count // BLOCK):
            received = recv_buf[pl.ds(first + block * BLOCK, BLOCK)]
            ordered.append(dot(into_ref[...], received.reshape(BLOCK * MSG, FEAT)))

        def rows_of(place):
            return jnp.concatenate([part[place * size : (place + 1) * size] for part in ordered], 0)

        rows = pl.ds(pl.multiple_of(first * CAP, 16), count * CAP)
        kept = slice(0, count * CAP)
        experts = range(LOCAL)
        for e in experts:
            act0[e, rows] = rows_of(e).astype(jnp.bfloat16)
            g_group[e, kept] = rows_of(LOCAL + e)
        val0 = [dot(act0[e, rows], wfull[e, 0]) for e in experts]
        for e in experts:
            sig = jax.nn.sigmoid(val0[e])
            act1[e, rows] = (val0[e] * sig).astype(jnp.bfloat16)
            slope0[e, kept] = slope(val0[e], sig)
        val1 = [dot(act1[e, rows], wfull[e, 1]) for e in experts]
        for e in experts:
            sig = jax.nn.sigmoid(val1[e])
            pre1[e, rows] = (g_group[e, kept] * slope(val1[e], sig)).astype(jnp.bfloat16)
        back1 = [dot_t(pre1[e, rows], wfull[e, 1]) for e in experts]
        for e in experts:
            grad = back1[e].astype(jnp.bfloat16).astype(jnp.float32)
            pre0[e, rows] = (grad * slope0[e, kept]).astype(jnp.bfloat16)
        back0 = [dot_t(pre0[e, rows], wfull[e, 0]) for e in experts]
        for block in range(count // BLOCK):
            part = slice(block * size, (block + 1) * size)
            by_expert = jnp.concatenate([back0[e][part] for e in experts], 0).astype(jnp.bfloat16)
            by_message = dot(back_ref[...], by_expert)
            for j in range(BLOCK):
                part = slice(j * PAIR, (j + 1) * PAIR)
                both = jnp.concatenate([by_message[part, :HALF], by_message[part, HALF:]], 0)
                ysend_buf[first + block * BLOCK + j] = both.astype(jnp.bfloat16)

        send_all(reply, first, 9)

    other_half = pl.ds(pl.multiple_of((1 - node) * HALF, HALF), HALF)

    def wg_copy(local):
        return pltpu.make_async_remote_copy(
            src_ref=wg_send.at[local],
            dst_ref=wg_recv.at[local],
            send_sem=gsend_sem.at[local],
            recv_sem=grecv_sem.at[local],
            device_id=(me, 1 - node),
            device_id_type=MESH,
        )

    layers = ((act0, pre0), (act1, pre1))
    span = EXPERT_ROWS // 2

    def first_grads(local, carry):
        for layer, (act, pre) in enumerate(layers):
            wg_acc[local, layer] = t_dot(act[local, :span], pre[local, :span])
        return carry

    def last_grads(local, carry):
        for layer, (act, pre) in enumerate(layers):
            for half, result in ((other_half, wg_send), (my_half, wg_own)):
                total = wg_acc[local, layer, half] + t_dot(
                    act[local, span:, half], pre[local, span:]
                )
                result[local, layer] = (total * norm_scale).astype(jnp.bfloat16)
        wg_copy(local).start()
        return carry

    def wg_store(local):
        return pltpu.make_async_copy(wg_out.at[local], wgrads_ref.at[local], out_sem.at[local])

    def add_grads(local, carry):
        wg_copy(local).wait()
        total = wg_own[local].astype(jnp.float32) + wg_recv[local].astype(jnp.float32)
        wg_out[local] = total.astype(jnp.bfloat16)
        wg_store(local).start()
        return carry

    def pass_of(step):
        compute(PASS, step * PASS)

        @pl.when(step == PEERS // PASS // 2 - 1)
        def _():
            lax.fori_loop(0, LOCAL, first_grads, 0)

    over(0, PEERS // PASS, pass_of)
    lax.fori_loop(0, LOCAL, last_grads, 0)
    yrecv_buf[0] = ysend_buf[0]

    acc[...] = jnp.zeros_like(acc)

    def combined(group):
        for_group(group, lambda messages, replies: replies.wait_recv())
        received = yrecv_buf[pl.ds(group * GROUP, GROUP)].astype(jnp.float32)
        left = received[:, :PAIR].reshape(GROUP * PAIR, HALF)
        right = received[:, PAIR:].reshape(GROUP * PAIR, HALF)
        ordered = jnp.concatenate([left, right], 1).astype(jnp.bfloat16)
        columns = lax.broadcasted_iota(jnp.int32, (ROWS, GROUP * PAIR), 1) + group * (GROUP * PAIR)
        pick = (target_col[:, :1].astype(jnp.int32) == columns).astype(jnp.bfloat16)
        return dot(pick, ordered)

    def combine(group, carry):
        acc[...] += combined(group)
        return carry

    lax.fori_loop(0, GROUPS - 1, combine, 0)
    lax.fori_loop(0, LOCAL, add_grads, 0)
    g_out[...] = (acc[...] + combined(GROUPS - 1)).astype(jnp.bfloat16)
    g_store = pltpu.make_async_copy(g_out, grads_ref, gout_sem)
    g_store.start()

    def drain(group):
        for_group(group, lambda messages, replies: messages.wait_send())
        for_group(group, lambda messages, replies: replies.wait_send())

    over(0, GROUPS, drain)
    over(0, LOCAL, lambda local: wg_store(local).wait())
    g_store.wait()


def hand_over(grads_in, wgrads_in, grads_out, wgrads_out, grads_buf, wgrads_buf, in_sem, out_sem):
    size = ROWS // GRAD_PARTS
    rows = [pl.ds(k * size, size) for k in range(GRAD_PARTS)]
    parts = [
        (src.at[part], buf.at[part], dst.at[part])
        for src, buf, dst, all_parts in (
            (wgrads_in, wgrads_buf, wgrads_out, [(k, j) for k in range(LOCAL) for j in range(2)]),
            (grads_in, grads_buf, grads_out, rows),
        )
        for part in all_parts
    ]
    reads = [pltpu.make_async_copy(p[0], p[1], in_sem.at[k]) for k, p in enumerate(parts)]
    writes = [pltpu.make_async_copy(p[1], p[2], out_sem.at[k]) for k, p in enumerate(parts)]
    for copy in reads:
        copy.start()
    for read, write in zip(reads, writes):
        read.wait()
        write.start()
    for copy in writes:
        copy.wait()


def on_device(samples, cotangent, weights, expert_ids):
    bf16 = jnp.bfloat16
    node_count = lax.axis_size("node")
    norm_scale = 1.0 / math.sqrt(ROWS * node_count / LOCAL)
    hbm = pl.BlockSpec(memory_space=pltpu.HBM)
    outs = (
        jax.ShapeDtypeStruct((ROWS, FEAT), bf16),
        jax.ShapeDtypeStruct((LOCAL, 2, HALF, FEAT), bf16),
    )
    results = pl.pallas_call(
        functools.partial(kernel, norm_scale),
        out_shape=outs,
        in_specs=[hbm] * 4,
        out_specs=(hbm, hbm),
        scratch_shapes=[
            pltpu.VMEM((1, ROWS), jnp.int32),
            pltpu.VMEM((ROWS, FEAT), bf16),
            pltpu.VMEM((ROWS, FEAT), bf16),
            pltpu.VMEM((BLOCK * MSG, BLOCK * MSG), bf16),
            pltpu.VMEM((BLOCK * PAIR, BLOCK * PAIR), bf16),
            pltpu.VMEM((PEERS, MSG, FEAT), bf16),
            pltpu.VMEM((PEERS, MSG, FEAT), bf16),
            pltpu.VMEM((PEERS, MSG, HALF), bf16),
            pltpu.VMEM((PEERS, MSG, HALF), bf16),
            pltpu.VMEM((LOCAL, GROUP_ROWS, FEAT), jnp.float32),
            pltpu.VMEM((LOCAL, GROUP_ROWS, FEAT), jnp.float32),
            pltpu.VMEM((LOCAL, EXPERT_ROWS, FEAT), bf16),
            pltpu.VMEM((LOCAL, EXPERT_ROWS, FEAT), bf16),
            pltpu.VMEM((LOCAL, EXPERT_ROWS, FEAT), bf16),
            pltpu.VMEM((LOCAL, EXPERT_ROWS, FEAT), bf16),
            pltpu.VMEM((LOCAL, 2, FEAT, FEAT), bf16),
            pltpu.VMEM((LOCAL, 2, FEAT, FEAT), jnp.float32),
            pltpu.VMEM((LOCAL, 2, HALF, FEAT), bf16),
            pltpu.VMEM((LOCAL, 2, HALF, FEAT), bf16),
            pltpu.VMEM((LOCAL, 2, HALF, FEAT), bf16),
            pltpu.VMEM((LOCAL, 2, HALF, FEAT), bf16),
            pltpu.VMEM((ROWS, FEAT), bf16),
            pltpu.VMEM((ROWS, 128), jnp.float32),
            pltpu.VMEM((ROWS, FEAT), jnp.float32),
            pltpu.SemaphoreType.DMA((3,)),
            pltpu.SemaphoreType.DMA((GROUPS,)),
            pltpu.SemaphoreType.DMA((GROUPS,)),
            pltpu.SemaphoreType.DMA((GROUPS,)),
            pltpu.SemaphoreType.DMA((GROUPS,)),
            pltpu.SemaphoreType.DMA,
            pltpu.SemaphoreType.DMA,
            pltpu.SemaphoreType.DMA,
            pltpu.SemaphoreType.DMA((LOCAL,)),
            pltpu.SemaphoreType.DMA((LOCAL,)),
            pltpu.SemaphoreType.DMA((LOCAL,)),
            pltpu.SemaphoreType.DMA,
        ],
        compiler_params=pltpu.CompilerParams(
            collective_id=0, has_side_effects=True, vmem_limit_bytes=60 * 1024 * 1024
        ),
    )(
        expert_ids.reshape(1, ROWS),
        samples,
        cotangent,
        weights,
    )
    return pl.pallas_call(
        hand_over,
        out_shape=outs,
        in_specs=[hbm] * 2,
        out_specs=(hbm, hbm),
        scratch_shapes=[
            pltpu.VMEM((ROWS, FEAT), bf16),
            pltpu.VMEM((LOCAL, 2, HALF, FEAT), bf16),
            pltpu.SemaphoreType.DMA((2 * LOCAL + GRAD_PARTS,)),
            pltpu.SemaphoreType.DMA((2 * LOCAL + GRAD_PARTS,)),
        ],
        compiler_params=pltpu.CompilerParams(vmem_limit_bytes=60 * 1024 * 1024),
    )(*results)


def solution(mesh):
    return jax.shard_map(
        on_device,
        mesh=mesh,
        in_specs=(
            P(("expert", "node"), None),
            P(("expert", "node"), None),
            P("expert", None, "node", None),
            P(("expert", "node"), None),
        ),
        out_specs=(P(("expert", "node"), None), P("expert", None, "node", None)),
        check_vma=False,
    )
```
